128 devices in a mesh: slab: 8 (over z, core), row: 16 (over x, y).
Axes of the slice: x: 4, y: 4, z: 4, core: 2. Of those that a mesh axis runs over, the one named last changes fastest.
Arguments:
- moving: bfloat16 [16, 1024, 1024], P('slab', 'row'), may hold values from -6 to 6
- fixed: float32 [16, 1024, 1024], P('slab', 'row'), may hold values from -18 to 18
- requests: int32 [8, 16, 128, 2], P('slab', 'row'), may hold values from -1 to 31, as said below
- footpoints: int32 [8, 16, 32, 8], P('slab', 'row'), may hold values from 0 to 255, as said below
- offset_x: int32 [8, 16, 32], P('slab', 'row'), may hold values from 0 to 1
- offset_y: int32 [8, 16, 32], P('slab', 'row'), may hold values from 0 to 15
- offset_z: int32 [8, 16, 32], P('slab', 'row'), may hold values from 0 to 127
- fractions: float32 [8, 16, 32, 3], P('slab', 'row'), may hold values from 0 to 1
Outputs:
- solution: float32 [3, 16, 1024, 1024], P(None, 'slab', 'row')
- residual: float32 [3, 16, 1024, 1024], P(None, 'slab', 'row')
The draws below stay inside these ranges and needn't reach their ends.
Inputs may be any that keep to these rules, and one draw needn't show every extreme that they name: `requests`: used slots come first for each device and peer, empty ones hold -1; every device asks some peer for all 2 slots. `footpoints`: entries are slots p * 2 + c with requests[device, p, c] not -1, and every such slot of the device is named.
All inputs are finite; a program needn't handle non-finite values.
Results may differ from the reference program's by a relative error of at most 0.0095.
Values may be sent and summed in bfloat16 or wider, within the bound.
No kernel may reach another device: no remote copies, remote signals or barrier semaphores. Data moves between devices by JAX's collectives and lax.ppermute only.
A program may use at most 64 MiB of HBM per device.

```python
import jax
import jax.numpy as jnp
from jax import lax

CX = 2
CY = 64
CZ = 1024
TY = 16
TZ = 128
CAP = 2
ITERS = 4
NX = 16
NY = 1024
NZ = 1024
SLAB_DEVS = 8
ROW_DEVS = 16
PEERS = 128
TILES_DEV = 32
N_SLAB = 8
N_ROW = 16


def shared_plan(key):
    keys = jax.random.split(key, 4)
    counts = jax.random.randint(keys[0], (PEERS, PEERS), 0, CAP + 1)
    forced = jax.random.randint(keys[1], (PEERS,), 1, PEERS)
    peer_ids = jnp.arange(PEERS, dtype=jnp.int32)
    counts = jnp.where(peer_ids[None, :] == forced[:, None], CAP, counts)
    first_dev = (peer_ids == 0)[:, None]
    last_dev = (peer_ids == PEERS - 1)[:, None]
    last_peer = (peer_ids == PEERS - 1)[None, :]
    first_peer = (peer_ids == 0)[None, :]
    counts = jnp.where(first_dev & last_peer, CAP, counts)
    counts = jnp.where(last_dev & first_peer, 0, counts)
    slot_ids = jnp.arange(CAP, dtype=jnp.int32)
    filled = slot_ids[None, None, :] < counts[:, :, None]
    numbers = jax.random.randint(keys[2], (PEERS, PEERS, CAP), 0, TILES_DEV)
    top_entry = (first_dev & last_peer)[:, :, None] & (slot_ids == 0)[None, None, :]
    numbers = jnp.where(top_entry, TILES_DEV - 1, numbers)
    requests = jnp.where(filled, numbers, -1).astype(jnp.int32)
    flat_filled = filled.reshape(PEERS, PEERS * CAP).astype(jnp.int32)
    order = jnp.argsort(1 - flat_filled, axis=1, stable=True).astype(jnp.int32)
    totals = jnp.sum(flat_filled, axis=1)
    perms = jax.vmap(lambda one: jax.random.permutation(one, 8 * TILES_DEV))(jax.random.split(keys[3], PEERS))
    chosen = (perms.astype(jnp.int32) % totals[:, None]).astype(jnp.int32)
    footpoints = jnp.take_along_axis(order, chosen, axis=1).astype(jnp.int32)
    return (requests.reshape(SLAB_DEVS, ROW_DEVS, PEERS, CAP), footpoints.reshape(SLAB_DEVS, ROW_DEVS, TILES_DEV, 8))


def draw_requests(key, part):
    shared = shared_plan(key)
    return shared[0]


def draw_footpoints(key, part):
    shared = shared_plan(key)
    return shared[1]


def draw_fixed(key, part):
    key = jax.random.fold_in(key, 11)
    ramp = 1.0 + 2.0 * jnp.arange(NX, dtype=jnp.float32) / max(NX - 1, 1)
    base = jnp.clip(jax.random.normal(key, (NX, NY, NZ), jnp.float32), -6.0, 6.0)
    return (base * ramp[:, None, None]).astype(jnp.float32)


def set_ends(entries, key, least, largest):
    place = [jax.random.randint(jax.random.fold_in(key, axis), (), 0, length) for axis, length in enumerate(entries.shape)]
    main_axis = entries.shape.index(max(entries.shape))
    neighbour = place[:main_axis] + [(place[main_axis] + 1) % entries.shape[main_axis]] + place[main_axis + 1:]
    return entries.at[tuple(place)].set(least).at[tuple(neighbour)].set(largest)


def steps_of(rng, shape, cuts, smallest, top_value):
    level, own = 1.0, jax.random.fold_in(rng, 6)
    for dim, shards_of in cuts:
        draws = jnp.exp(jax.random.uniform(jax.random.fold_in(own, dim), (shards_of,), jnp.float32, smallest / len(cuts), top_value / len(cuts)))
        level = level * jnp.repeat(draws, shape[dim] // shards_of).reshape([-1 if axis == dim else 1 for axis in range(len(shape))])
    return level


def centred(own_key, dims, spread, limit, shards=(), kind=jnp.bfloat16):
    gain = steps_of(own_key, dims, shards, -0.22, 0.18) if shards else 1.0
    drawn = jax.random.normal(own_key, dims, jnp.float32) * spread * gain
    return jnp.minimum(jnp.maximum(drawn, -limit), limit).astype(kind)


def setup_inputs(seed: int = 0) -> dict:
    key_list = jax.random.split(jax.random.key(seed), 9)
    moving = centred(key_list[0], (NX, NY, NZ), 1.0, 6.0, ((0, 8), (1, 16)))
    fixed = draw_fixed(jax.random.fold_in(key_list[8], 71), 0)
    requests = draw_requests(jax.random.fold_in(key_list[8], 71), 0)
    footpoints = draw_footpoints(jax.random.fold_in(key_list[8], 71), 0)
    offset_x = set_ends(jax.random.randint(key_list[4], (SLAB_DEVS, ROW_DEVS, TILES_DEV), 0, CX), jax.random.fold_in(key_list[4], 1), 0, CX - 1).astype(jnp.int32)
    offset_y = set_ends(jax.random.randint(key_list[5], (SLAB_DEVS, ROW_DEVS, TILES_DEV), 0, TY), jax.random.fold_in(key_list[5], 1), 0, TY - 1).astype(jnp.int32)
    offset_z = set_ends(jax.random.randint(key_list[6], (SLAB_DEVS, ROW_DEVS, TILES_DEV), 0, TZ), jax.random.fold_in(key_list[6], 1), 0, TZ - 1).astype(jnp.int32)
    fractions = jnp.clip(1.0 * jax.random.uniform(key_list[7], (SLAB_DEVS, ROW_DEVS, TILES_DEV, 3), jnp.float32) ** steps_of(key_list[7], (SLAB_DEVS, ROW_DEVS, TILES_DEV, 3), ((0, 8), (1, 16)), -0.2, 0.2), 0.0, 1.0)
    return {"moving": moving, "fixed": fixed, "requests": requests, "footpoints": footpoints, "offset_x": offset_x, "offset_y": offset_y, "offset_z": offset_z, "fractions": fractions}


smoothing = 0.02
damping = 0.1
stencil_diag = 42.0


def weights(offset, fraction, length):
    inside = jnp.arange(length, dtype=jnp.int32)[None, :, None]
    source = jnp.arange(2 * length, dtype=jnp.int32)[None, None, :]
    anchor = offset.astype(jnp.int32)[:, None, None] + inside
    portion = fraction[:, None, None]
    table = jnp.where(source == anchor, 1.0 - portion, 0.0) + jnp.where(source == anchor + 1, portion, 0.0)
    return table.astype(jnp.bfloat16)


def assemble(arrived, corner):
    count = corner.shape[0]
    depth, height, width = arrived.shape[1], arrived.shape[2], arrived.shape[3]
    picked = arrived[corner.reshape(-1)]
    picked = picked.reshape(count, 2, 2, 2, depth, height, width).transpose(0, 1, 4, 2, 5, 3, 6)
    return picked.reshape(count, 2 * depth, 2 * height, 2 * width)


def interpolate(patch, shift_x, shift_y, shift_z, fraction):
    depth = patch.shape[1] // 2
    height = patch.shape[2] // 2
    width = patch.shape[3] // 2
    weight_z = weights(shift_z, fraction[:, 2], width).astype(jnp.float32)
    weight_y = weights(shift_y, fraction[:, 1], height).astype(jnp.float32)
    weight_x = weights(shift_x, fraction[:, 0], depth).astype(jnp.float32)
    first = jnp.einsum("tabk,tzk->tabz", patch.astype(jnp.float32), weight_z).astype(jnp.bfloat16)
    second = jnp.einsum("tabz,tyb->tayz", first.astype(jnp.float32), weight_y).astype(jnp.bfloat16)
    return jnp.einsum("tayz,txa->txyz", second.astype(jnp.float32), weight_x)


def laplace(field):
    padded = jnp.pad(field, ((0, 0), (1, 1), (1, 1), (1, 1)))
    beside = padded[:, 2:, 1:-1, 1:-1] + padded[:, :-2, 1:-1, 1:-1]
    beside = beside + padded[:, 1:-1, 2:, 1:-1] + padded[:, 1:-1, :-2, 1:-1]
    beside = beside + padded[:, 1:-1, 1:-1, 2:] + padded[:, 1:-1, 1:-1, :-2]
    return 6.0 * field - beside


def reference(moving, fixed, requests, footpoints, offset_x, offset_y, offset_z, fractions):
    across = CY // TY
    along = CZ // TZ
    tile_set = moving.reshape(N_SLAB, CX, N_ROW, across, TY, along, TZ).transpose(0, 2, 3, 5, 1, 4, 6)
    tile_set = tile_set.reshape(PEERS, TILES_DEV, CX, TY, TZ)
    peer_ids = jnp.arange(PEERS, dtype=jnp.int32)

    def one_device(items):
        asked, corner, shift_x, shift_y, shift_z, fraction = items
        picked = tile_set[peer_ids[:, None], jnp.maximum(asked, 0)]
        picked = jnp.where((asked >= 0)[:, :, None, None, None], picked, jnp.zeros_like(picked))
        arrived = picked.reshape(PEERS * CAP, CX, TY, TZ)
        patch = assemble(arrived, corner)
        warped_tiles = interpolate(patch, shift_x, shift_y, shift_z, fraction)
        return warped_tiles.reshape(across, along, CX, TY, TZ).transpose(2, 0, 3, 1, 4).reshape(CX, CY, CZ)

    blocks = lax.map(one_device, (requests.reshape(PEERS, PEERS, CAP), footpoints.reshape(PEERS, TILES_DEV, 8),
                                  offset_x.reshape(PEERS, TILES_DEV), offset_y.reshape(PEERS, TILES_DEV),
                                  offset_z.reshape(PEERS, TILES_DEV), fractions.reshape(PEERS, TILES_DEV, 3)))
    warped = blocks.reshape(N_SLAB, N_ROW, CX, CY, CZ).transpose(0, 2, 1, 3, 4).reshape(NX, NY, NZ)
    padded = jnp.pad(warped, 1)
    slope = jnp.stack([(padded[2:, 1:-1, 1:-1] - padded[:-2, 1:-1, 1:-1]) * 0.5,
                       (padded[1:-1, 2:, 1:-1] - padded[1:-1, :-2, 1:-1]) * 0.5,
                       (padded[1:-1, 1:-1, 2:] - padded[1:-1, 1:-1, :-2]) * 0.5])
    rhs = -slope * (warped - fixed)[None]
    precond = slope * slope + stencil_diag * smoothing + damping

    def operate(field):
        return slope * jnp.sum(slope * field, axis=0)[None] + smoothing * laplace(laplace(field)) + damping * field

    solution = jnp.zeros_like(rhs)
    residual = rhs
    prepared = residual / precond
    direction = prepared
    norm_now = jnp.sum(residual * prepared)
    for step in range(ITERS):
        image = operate(direction)
        alpha = norm_now / jnp.sum(direction * image)
        solution = solution + alpha * direction
        residual = residual - alpha * image
        prepared = residual / precond
        norm_next = jnp.sum(residual * prepared)
        direction = prepared + (norm_next / norm_now) * direction
        norm_now = norm_next
    return solution, residual
```

```python
import functools

import jax
import jax.numpy as jnp
from jax import lax
from jax.experimental import pallas as pl
from jax.experimental.pallas import tpu as pltpu
from jax.sharding import PartitionSpec as P

TY = 16
TZ = 128
ITERS = 4

smoothing = 0.02
damping = 0.1
stencil_diag = 42.0

LOW = 0.1
HIGH = 3.2
CENTRE = (HIGH + LOW) / 2
HALF = (HIGH - LOW) / 2

BOTH = ("slab", "row")
F32 = jnp.float32
BF16 = jnp.bfloat16


def spread(width):
    source = lax.broadcasted_iota(jnp.int32, (width, width), 0)
    target = lax.broadcasted_iota(jnp.int32, (width, width), 1)
    return (target == (source % 8) * (width // 8) + source // 8).astype(BF16)


def warp_kernel(foot, ox, oy, oz, wts, arrived, fixed, perm, out, nat):
    base_z = lax.broadcasted_iota(jnp.int32, (256, 128), 0) - lax.broadcasted_iota(jnp.int32, (256, 128), 1)
    ro = lax.broadcasted_iota(jnp.int32, (64, 128), 0)
    ci = lax.broadcasted_iota(jnp.int32, (64, 128), 1)
    same = (ro // 32 == ci // 64) & ((ro // 16) % 2 == (ci // 16) % 2)
    base_y = jnp.where(same, ((ci // 32) % 2) * 16 + ci % 16 - ro % 16, -1000)

    def band(base, shift, here, after):
        return jnp.where(base == shift, here, jnp.where(base == shift + 1, after, 0.0)).astype(BF16)

    def tile_row(j, carry):
        for k in range(8):
            t = j * 8 + k
            sides = []
            for c in range(2):
                sides.append(
                    jnp.concatenate(
                        [arrived[foot[t * 8 + 4 * a + 2 * b + c]] for a in range(2) for b in range(2)], axis=0
                    )
                )
            patch = jnp.concatenate(sides, axis=1)
            wz = band(base_z, oz[t], wts[t * 6 + 4], wts[t * 6 + 5])
            first = jnp.dot(patch, wz, preferred_element_type=F32).astype(BF16)
            wy = band(base_y, oy[t], wts[t * 6 + 2], wts[t * 6 + 3])
            second = jnp.dot(wy, first, preferred_element_type=F32).astype(BF16).astype(F32)
            shift = ox[t]
            for xo in range(2):
                total = None
                for p in range(xo, xo + 3):
                    weight = jnp.where(
                        p - xo == shift, wts[t * 6], jnp.where(p - xo == shift + 1, wts[t * 6 + 1], 0.0)
                    )
                    term = weight * second[p * 16 : (p + 1) * 16]
                    total = term if total is None else total + term
                rows = pl.ds(pl.multiple_of(j * 16, 16), 16)
                lanes = slice(k * 128, (k + 1) * 128)
                nat[xo, rows, lanes] = total.astype(BF16)
                nat[2 + xo, rows, lanes] = (total - fixed[xo, rows, lanes]).astype(BF16)
        return carry

    lax.fori_loop(0, 4, tile_row, 0)
    mixed = jnp.dot(nat[...].reshape(256, 1024), perm[...], preferred_element_type=F32)
    out[...] = mixed.astype(BF16).reshape(4, 64, 1024)


def warp(arrived, footpoints, offset_x, offset_y, offset_z, fractions, fixed, perm):
    near = lax.reduce_precision(1.0 - fractions, 8, 7)
    far = lax.reduce_precision(fractions, 8, 7)
    wts = jnp.stack([near, far], axis=-1).reshape(-1)
    smem = pl.BlockSpec(memory_space=pltpu.SMEM)
    vmem = pl.BlockSpec(memory_space=pltpu.VMEM)
    return pl.pallas_call(
        warp_kernel,
        out_shape=jax.ShapeDtypeStruct((4, 64, 1024), BF16),
        in_specs=[smem] * 5 + [vmem] * 3,
        out_specs=vmem,
        scratch_shapes=[pltpu.VMEM((4, 64, 1024), BF16)],
        compiler_params=pltpu.CompilerParams(vmem_limit_bytes=32 * 1024 * 1024),
        name="warp",
    )(footpoints.reshape(-1), offset_x, offset_y, offset_z, wts, arrived, fixed, perm)


def edge_masks():
    sub = lax.broadcasted_iota(jnp.int32, (1, 8, 128), 1)
    lane = lax.broadcasted_iota(jnp.int32, (1, 8, 128), 2)
    one = lambda flag: jnp.where(flag, 1.0, 0.0).astype(F32)
    return one(sub != 0), one(sub != 7), one(lane != 0), one(lane != 127)


def x_pair(v0, v1, masks):
    return pltpu.roll(v1, 1, 1) * masks[0], pltpu.roll(v0, 7, 1) * masks[1]


def z_pair(v, masks):
    before = jnp.concatenate([pltpu.roll(v[7:8], 1, 2) * masks[2], v[:7]], axis=0)
    after = jnp.concatenate([v[1:], pltpu.roll(v[:1], 127, 2) * masks[3]], axis=0)
    return before, after


def beside(v0, v1, masks):
    before, after = x_pair(v0, v1, masks)
    a0, b0 = z_pair(v0, masks)
    a1, b1 = z_pair(v1, masks)
    return (v1 + before) + (a0 + b0), (v0 + after) + (a1 + b1)


K_LO = slice(0, 8)
K_HI = slice(8, 16)


def krylov_kernel(rowmask, arr, mom, vout, sout, d_s, w_s, s_s, im_s, u_s, v0, v1, v2, v3, v4, sems):
    vs = [v0, v1, v2, v3, v4]
    masks = edge_masks()
    for src in range(8):
        lines = arr[src].astype(F32).reshape(104, 1024)
        for kz in range(8):
            d_s[kz, src * 104 : (src + 1) * 104, :] = lines[:, kz * 128 : (kz + 1) * 128]

    def fetch(row):
        return [d_s[kz, pl.ds(row, 8, stride=104), :] for kz in range(8)]

    def put_w(i, row0, row1):
        for kx, row in ((0, row0), (1, row1)):
            for kz, vreg in enumerate(fetch(row)):
                w_s[i, kx * 8 + kz] = vreg

    put_w(0, 96, 98)
    put_w(25, 97, 99)

    def fill(n, carry):
        put_w(n + 1, 48 + n, 72 + n)
        return carry

    lax.fori_loop(0, 24, fill, 0)

    def begin(n, carry):
        w0, w1 = w_s[n + 1, K_LO], w_s[n + 1, K_HI]
        before, after = x_pair(w0, w1, masks)
        keep = rowmask[n]
        for kx, w, xs in ((0, w0, w1 - before), (1, w1, after - w0)):
            part = slice(kx * 8, kx * 8 + 8)
            diff = jnp.stack(fetch(n + 24 * kx))
            zb, za = z_pair(w, masks)
            ys = w_s[n + 2, part] - w_s[n, part]
            for c, s in enumerate((xs * 0.5, ys * 0.5, (za - zb) * 0.5)):
                im = keep / (s * s + (stencil_diag * smoothing + damping))
                s_s[c, n, part] = s
                im_s[c, n, part] = im
                v0[c, n, part] = -s * diff * im
        return carry

    lax.fori_loop(0, 24, begin, 0)

    def copy(j):
        return pltpu.make_async_copy(vs[j].at[:, pl.ds(8 - 2 * j, 8)], vout.at[j], sems.at[j])

    s_copy = pltpu.make_async_copy(s_s.at[:, pl.ds(8, 8)], sout, sems.at[5])
    s_copy.start()
    copy(0).start()

    for j in range(4):
        gain = (1.0 if j == 0 else 2.0) / HALF
        old, new = vs[j], vs[j + 1]
        off = 2 * j

        def first(n, carry):
            scale = rowmask[n] * (gain * smoothing)
            for c in range(3):
                a0, a1 = old[c, n - off, K_LO], old[c, n - off, K_HI]
                b0, b1 = beside(a0, a1, masks)
                for part, a, b in ((K_LO, a0, b0), (K_HI, a1, b1)):
                    total = b + (old[c, n - off - 1, part] + old[c, n - off + 1, part])
                    u_s[c, n - 1, part] = (6.0 * a - total) * scale
            return carry

        lax.fori_loop(off + 1, 23 - off, first, 0)

        def second(n, carry):
            dots = []
            for part in (K_LO, K_HI):
                dot = s_s[0, n, part] * old[0, n - off, part]
                dot = dot + s_s[1, n, part] * old[1, n - off, part]
                dots.append((dot + s_s[2, n, part] * old[2, n - off, part]) * gain)
            for c in range(3):
                a0, a1 = u_s[c, n - 1, K_LO], u_s[c, n - 1, K_HI]
                b0, b1 = beside(a0, a1, masks)
                for part, a, b, dot in ((K_LO, a0, b0, dots[0]), (K_HI, a1, b1, dots[1])):
                    total = b + (u_s[c, n - 2, part] + u_s[c, n, part])
                    v = old[c, n - off, part]
                    image = s_s[c, n, part] * dot + (6.0 * a - total) + (gain * damping) * v
                    value = im_s[c, n, part] * image - (gain * CENTRE) * v
                    if j > 0:
                        value = value - vs[j - 1][c, n - off + 2, part]
                    new[c, n - off - 2, part] = value
            return carry

        lax.fori_loop(off + 2, 22 - off, second, 0)
        copy(j + 1).start()

    def products(n, sums):
        sums = list(sums)
        for c in range(3):
            for part in (K_LO, K_HI):
                s = s_s[c, n, part]
                m = s * s + (stencil_diag * smoothing + damping)
                v = [vs[j][c, n - 2 * j, part] for j in range(5)]
                for j in range(4):
                    t = m * v[j]
                    for k, other in ((2 * j, v[j]), (2 * j + 1, v[j + 1])):
                        sums[k] = sums[k] + jnp.sum(t * other, axis=0)
        return tuple(sums)

    sums = lax.fori_loop(8, 16, products, tuple(jnp.zeros((8, 128), F32) for _ in range(8)))
    lane = lax.broadcasted_iota(jnp.int32, (1, 128), 1)
    line = jnp.zeros((1, 128), F32)
    for k in range(8):
        line = jnp.where(lane == k, jnp.sum(sums[k], keepdims=True), line)
    mom[...] = jnp.broadcast_to(line, mom.shape)
    s_copy.wait()
    for j in range(5):
        copy(j).wait()


def krylov(received, rowmask, peers):
    vmem = pl.BlockSpec(memory_space=pltpu.VMEM)
    hbm = pl.BlockSpec(memory_space=pl.ANY)

    def field(rows):
        return pltpu.VMEM((3, rows, 16, 8, 128), F32)

    return pl.pallas_call(
        krylov_kernel,
        out_shape=(
            jax.ShapeDtypeStruct((peers, 128), F32),
            jax.ShapeDtypeStruct((5, 3, 8, 16, 8, 128), F32),
            jax.ShapeDtypeStruct((3, 8, 16, 8, 128), F32),
        ),
        in_specs=[pl.BlockSpec(memory_space=pltpu.SMEM), vmem],
        out_specs=(vmem, hbm, hbm),
        scratch_shapes=[
            pltpu.VMEM((8, 832, 128), F32),
            pltpu.VMEM((26, 16, 8, 128), F32),
            field(24),
            field(24),
            field(22),
            field(24),
            field(20),
            field(16),
            field(12),
            field(8),
            pltpu.SemaphoreType.DMA((6,)),
        ],
        compiler_params=pltpu.CompilerParams(vmem_limit_bytes=50 * 1024 * 1024),
        name="krylov",
    )(rowmask, received)


def coefficients(m):
    def lam(k):
        if k == 0:
            return CENTRE * m[0] + HALF * m[1]
        return CENTRE * m[k] + (HALF / 2) * (m[k + 1] + m[k - 1])

    lams = [lam(k) for k in range(7)]
    rows = [[0.5 * (lams[i + j] + lams[abs(i - j)]) for j in range(4)] + [m[i]] for i in range(4)]
    for p in range(4):
        inverse = 1.0 / rows[p][p]
        for q in range(p + 1, 4):
            factor = rows[q][p] * inverse
            rows[q] = [rows[q][k] - factor * rows[p][k] if k > p else rows[q][k] for k in range(5)]
    part = [None] * 4
    for p in reversed(range(4)):
        value = rows[p][4]
        for q in range(p + 1, 4):
            value = value - rows[p][q] * part[q]
        part[p] = value / rows[p][p]
    rest = [1.0 - CENTRE * part[0] - (HALF / 2) * part[1]]
    rest.append(-CENTRE * part[1] - HALF * part[0] - (HALF / 2) * part[2])
    rest.append(-CENTRE * part[2] - (HALF / 2) * (part[1] + part[3]))
    rest.append(-CENTRE * part[3] - (HALF / 2) * part[2])
    rest.append(-(HALF / 2) * part[3])
    return part, rest


def combine_kernel(mom, v, s, out, turn):
    line = jnp.sum(mom[...], axis=0, keepdims=True)
    lane = lax.broadcasted_iota(jnp.int32, (1, 128), 1)
    p = [jnp.sum(jnp.where(lane == k, line, 0.0), axis=1, keepdims=True) for k in range(8)]
    m = [p[0], p[1]] + [2.0 * p[k] - p[k % 2] for k in range(2, 8)]
    part, rest = coefficients(m)
    part = [jnp.broadcast_to(x, (8, 128)) for x in part]
    rest = [jnp.broadcast_to(x, (8, 128)) for x in rest]

    def row(i, carry):
        for kx in range(2):
            at = pl.ds(pl.multiple_of((kx * 8 + i) * 8, 8), 8)
            for kz in range(8):
                k = kx * 8 + kz
                vecs = [v[j, 0, i, k] for j in range(5)]
                slope = s[0, i, k]
                weight = slope * slope + (stencil_diag * smoothing + damping)
                turn[0, kz, at, :] = sum(part[j] * vecs[j] for j in range(4))
                turn[1, kz, at, :] = weight * sum(rest[j] * vecs[j] for j in range(5))
        return carry

    lax.fori_loop(0, 8, row, 0)
    for q in range(2):
        for dest in range(8):
            for kz in range(8):
                lanes = slice(kz * 128, kz * 128 + 128)
                out[dest, q, 0, :, lanes] = turn[q, kz, pl.ds(dest, 16, stride=8), :].astype(BF16)


def combine(moments, vectors, slopes):
    peers = moments.shape[0]
    return pl.pallas_call(
        combine_kernel,
        grid=(3,),
        out_shape=jax.ShapeDtypeStruct((8, 2, 3, 16, 1024), BF16),
        in_specs=[
            pl.BlockSpec((peers, 128), lambda c: (0, 0)),
            pl.BlockSpec((5, 1, 8, 16, 8, 128), lambda c: (0, c, 0, 0, 0, 0)),
            pl.BlockSpec((1, 8, 16, 8, 128), lambda c: (c, 0, 0, 0, 0)),
        ],
        out_specs=pl.BlockSpec((8, 2, 1, 16, 1024), lambda c: (0, 0, c, 0, 0)),
        scratch_shapes=[pltpu.VMEM((2, 8, 128, 128), F32)],
        compiler_params=pltpu.CompilerParams(vmem_limit_bytes=32 * 1024 * 1024),
        name="combine",
    )(moments, vectors, slopes)


def finish_kernel(back, perm, sol, res):
    for q, out in ((0, sol), (1, res)):
        lines = jnp.concatenate([back[src, q, 0] for src in range(8)], axis=0)
        cells = lax.dot_general(lines, perm[...], (((1,), (1,)), ((), ())), preferred_element_type=F32)
        for src in range(8):
            for kx in range(2):
                out[0, kx, src * 8 : src * 8 + 8, :] = cells[src * 16 + kx * 8 : src * 16 + kx * 8 + 8]


def finish(back, perm):
    shape = jax.ShapeDtypeStruct((3, 2, 64, 1024), F32)
    spec = pl.BlockSpec((1, 2, 64, 1024), lambda c: (c, 0, 0, 0))
    return pl.pallas_call(
        finish_kernel,
        grid=(3,),
        out_shape=(shape, shape),
        in_specs=[
            pl.BlockSpec((8, 2, 1, 16, 1024), lambda c: (0, 0, c, 0, 0)),
            pl.BlockSpec((1024, 1024), lambda c: (0, 0)),
        ],
        out_specs=(spec, spec),
        compiler_params=pltpu.CompilerParams(vmem_limit_bytes=32 * 1024 * 1024),
        name="finish",
    )(back, perm)


def windows(own):
    count = lax.axis_size("row")
    down = [(i, i + 1) for i in range(count - 1)]
    up = [(i + 1, i) for i in range(count - 1)]
    top = lax.ppermute(own[:, 55:64], "row", down)
    bottom = lax.ppermute(own[:, 0:9], "row", up)
    whole = jnp.concatenate([top, own, bottom], axis=1)
    pieces = []
    for s in range(8):
        body = whole[:, 8 * s + 1 : 8 * s + 25]
        ends = jnp.stack([whole[0, 8 * s], whole[0, 8 * s + 25], whole[1, 8 * s], whole[1, 8 * s + 25]])
        ends = jnp.concatenate([ends, jnp.zeros_like(ends)])
        pieces.append(
            jnp.concatenate([body[2:4].reshape(48, 1024), body[0:2].reshape(48, 1024), ends]).reshape(13, 8, 1024)
        )
    return jnp.stack(pieces)


def per_device(moving, fixed, requests, footpoints, offset_x, offset_y, offset_z, fractions):
    depth, height, width = moving.shape
    across = height // TY
    along = width // TZ
    perm = spread(width)
    tile_set = moving.reshape(depth, across, TY, along, TZ).transpose(1, 3, 0, 2, 4)
    tile_set = tile_set.reshape(across * along, depth, TY, TZ)
    asked = lax.all_to_all(requests[0, 0], BOTH, split_axis=0, concat_axis=0, tiled=True)
    peers, slots = asked.shape
    picked = jnp.take(tile_set, jnp.maximum(asked, 0).reshape(-1), axis=0)
    picked = picked.reshape(peers, slots, depth, TY, TZ)
    outgoing = jnp.where((asked >= 0)[:, :, None, None, None], picked, jnp.zeros_like(picked))
    arrived = lax.all_to_all(outgoing, BOTH, split_axis=0, concat_axis=0, tiled=True)
    arrived = arrived.reshape(peers * slots, depth * TY, TZ)
    own = warp(
        arrived, footpoints[0, 0], offset_x[0, 0], offset_y[0, 0], offset_z[0, 0], fractions[0, 0], fixed, perm
    )
    received = lax.all_to_all(windows(own), "slab", split_axis=0, concat_axis=0, tiled=True)
    start = lax.axis_index("row") * height + lax.axis_index("slab") * 8 - 8
    rows = start + jnp.arange(24, dtype=jnp.int32)
    rowmask = ((rows >= 0) & (rows < height * lax.axis_size("row"))).astype(F32)
    moments, vectors, slopes = krylov(received, rowmask, peers)
    moments = lax.all_to_all(moments, BOTH, split_axis=0, concat_axis=0, tiled=True)
    back = combine(moments, vectors, slopes)
    back = lax.all_to_all(back, "slab", split_axis=0, concat_axis=0, tiled=True)
    return finish(back, perm)


def solution(mesh):
    return jax.shard_map(
        per_device,
        mesh=mesh,
        in_specs=(
            P("slab", "row", None),
            P("slab", "row", None),
            P("slab", "row", None, None),
            P("slab", "row", None, None),
            P("slab", "row", None),
            P("slab", "row", None),
            P("slab", "row", None),
            P("slab", "row", None, None),
        ),
        out_specs=(P(None, "slab", "row", None), P(None, "slab", "row", None)),
        check_vma=False,
    )
```

```python
import functools

import jax
import jax.numpy as jnp
from jax import lax
from jax.experimental import pallas as pl
from jax.experimental.pallas import tpu as pltpu
from jax.sharding import PartitionSpec as P

TY = 16
TZ = 128
ITERS = 4

smoothing = 0.02
damping = 0.1
stencil_diag = 42.0

LOW = 0.1
HIGH = 3.2
CENTRE = (HIGH + LOW) / 2
HALF = (HIGH - LOW) / 2
REACH = (smoothing / HALF) ** 4 * 8

FINE = 4
WIDE = 8 // FINE
SPAN = 128 * FINE

BOTH = ("slab", "row")
F32 = jnp.float32
BF16 = jnp.bfloat16


def spread():
    source = lax.broadcasted_iota(jnp.int32, (SPAN, SPAN), 0)
    target = lax.broadcasted_iota(jnp.int32, (SPAN, SPAN), 1)
    return (target == (source % FINE) * 128 + source // FINE).astype(BF16)


def pick_kernel(asked, moving, out):
    depth = moving.shape[0]
    along = moving.shape[2] // TZ

    def peer(p, carry):
        for slot in range(out.shape[1]):
            number = asked[p, slot]
            tile = jnp.maximum(number, 0)
            rows = pl.ds(pl.multiple_of(lax.div(tile, along) * TY, TY), TY)
            lanes = pl.ds(pl.multiple_of(lax.rem(tile, along) * TZ, TZ), TZ)
            for x in range(depth):
                cells = moving[x, rows, lanes]
                out[p, slot, x] = jnp.where(number >= 0, cells, jnp.zeros_like(cells))
        return carry

    lax.fori_loop(0, out.shape[0], peer, 0, unroll=8)


def pick(asked, moving, slots):
    vmem = pl.BlockSpec(memory_space=pltpu.VMEM)
    return pl.pallas_call(
        pick_kernel,
        out_shape=jax.ShapeDtypeStruct((asked.shape[0], slots, moving.shape[0], TY, TZ), BF16),
        in_specs=[pl.BlockSpec(memory_space=pltpu.SMEM), vmem],
        out_specs=vmem,
        compiler_params=pltpu.CompilerParams(vmem_limit_bytes=8 * 1024 * 1024),
        name="pick",
    )(asked, moving)


def warp_kernel(foot, ox, oy, oz, wts, flip, arrived, fixed, perm, out, nat):
    base_z = lax.broadcasted_iota(jnp.int32, (256, 128), 0) - lax.broadcasted_iota(jnp.int32, (256, 128), 1)
    ro = lax.broadcasted_iota(jnp.int32, (64, 128), 0)
    ci = lax.broadcasted_iota(jnp.int32, (64, 128), 1)
    same = (ro // 32 == ci // 64) & ((ro // 16) % 2 == (ci // 16) % 2)
    base_y = jnp.where(same, ((ci // 32) % 2) * 16 + ci % 16 - ro % 16, -1000)

    def band(base, shift, here, after):
        return jnp.where(base == shift, here, jnp.where(base == shift + 1, after, 0.0)).astype(BF16)

    def tile_row(j, carry):
        for k in range(8):
            t = j * 8 + k
            sides = []
            for c in range(2):
                sides.append(
                    jnp.concatenate(
                        [arrived[foot[t * 8 + 4 * a + 2 * b + c]] for a in range(2) for b in range(2)], axis=0
                    )
                )
            patch = jnp.concatenate(sides, axis=1)
            wz = band(base_z, oz[t], wts[t * 6 + 4], wts[t * 6 + 5])
            first = jnp.dot(patch, wz, preferred_element_type=F32).astype(BF16)
            wy = band(base_y, oy[t], wts[t * 6 + 2], wts[t * 6 + 3])
            second = jnp.dot(wy, first, preferred_element_type=F32).astype(BF16).astype(F32)
            shift = ox[t]
            for xo in range(2):
                total = None
                for p in range(xo, xo + 3):
                    weight = jnp.where(
                        p - xo == shift, wts[t * 6], jnp.where(p - xo == shift + 1, wts[t * 6 + 1], 0.0)
                    )
                    term = weight * second[p * 16 : (p + 1) * 16]
                    total = term if total is None else total + term
                rows = pl.ds(pl.multiple_of(j * 16, 16), 16)
                lanes = slice(k * 128, (k + 1) * 128)
                nat[xo, rows, lanes] = total.astype(BF16)
                nat[2 + xo, rows, lanes] = (total - fixed[xo, rows, lanes]).astype(BF16)
        return carry

    lax.fori_loop(0, 4, tile_row, 0)
    for b in range(WIDE):
        lanes = slice(b * SPAN, b * SPAN + SPAN)
        mixed = jnp.dot(nat[:, :, lanes].reshape(256, SPAN), perm[...], preferred_element_type=F32)
        for place in range(8):
            dest = place + flip[0] * (7 - 2 * place)
            for m in range(4):
                out[dest, m, :, lanes] = mixed[m * 64 + place * 8 : m * 64 + place * 8 + 8].astype(BF16)


def warp(arrived, footpoints, offset_x, offset_y, offset_z, fractions, flip, fixed, perm):
    near = lax.reduce_precision(1.0 - fractions, 8, 7)
    far = lax.reduce_precision(fractions, 8, 7)
    wts = jnp.stack([near, far], axis=-1).reshape(-1)
    smem = pl.BlockSpec(memory_space=pltpu.SMEM)
    vmem = pl.BlockSpec(memory_space=pltpu.VMEM)
    return pl.pallas_call(
        warp_kernel,
        out_shape=jax.ShapeDtypeStruct((8, 4, 8, 1024), BF16),
        in_specs=[smem] * 6 + [vmem] * 3,
        out_specs=vmem,
        scratch_shapes=[pltpu.VMEM((4, 64, 1024), BF16)],
        compiler_params=pltpu.CompilerParams(vmem_limit_bytes=10 * 1024 * 1024),
        name="warp",
    )(footpoints.reshape(-1), offset_x, offset_y, offset_z, wts, flip, arrived, fixed, perm)


PARTS = [
    (kx, k, slice(kx * 8 + k * WIDE, kx * 8 + k * WIDE + WIDE)) for kx in range(2) for k in range(FINE)
]


def edge_masks():
    sub = lax.broadcasted_iota(jnp.int32, (1, 8, 128), 1)
    lane = lax.broadcasted_iota(jnp.int32, (WIDE, 8, 128), 2)
    one = lambda flag: jnp.where(flag, 1.0, 0.0).astype(F32)
    return one(sub != 0), one(sub != 7), lane == 0, lane == 127


def load(ref, *at):
    return {(kx, k): ref[(*at, tiles)] for kx, k, tiles in PARTS}


def x_pair(v, kx, k, masks):
    other = v[1 - kx, k]
    if kx == 0:
        return pltpu.roll(other, 1, 1) * masks[0], other
    return other, pltpu.roll(other, 7, 1) * masks[1]


def z_pair(v, kx, k, masks):
    nothing = jnp.zeros((1, 8, 128), F32)
    if k > 0:
        before = v[kx, k - 1]
    else:
        turned = pltpu.roll(v[kx, FINE - 1], 1, 2)
        carried = jnp.concatenate([nothing, turned[: WIDE - 1]], axis=0) if WIDE > 1 else nothing
        before = jnp.where(masks[2], carried, turned)
    if k < FINE - 1:
        after = v[kx, k + 1]
    else:
        turned = pltpu.roll(v[kx, 0], 127, 2)
        carried = jnp.concatenate([turned[1:], nothing], axis=0) if WIDE > 1 else nothing
        after = jnp.where(masks[3], carried, turned)
    return before, after


def beside(v, kx, k, masks):
    x0, x1 = x_pair(v, kx, k, masks)
    z0, z1 = z_pair(v, kx, k, masks)
    return (x0 + x1) + (z0 + z1)


def field(rows):
    return pltpu.VMEM((3, rows, 16, 8, 128), F32)


def krylov_kernel(rowmask, chunk3, mom, vout, sout, ends, s_s, im_s, v0, v1, v2, sems):
    masks = edge_masks()

    def chain(c, tiles, end, step):
        one = im_s[c, end, tiles] * im_s[c, end - step, tiles]
        return one * (im_s[c, end - 2 * step, tiles] * im_s[c, end - 3 * step, tiles]) * REACH

    def prepare(in_s, d_s, w_s, in_sems):
        chunks = [pltpu.make_async_copy(ref, in_s.at[g], in_sems.at[g]) for g, ref in enumerate((chunk3.at[0], chunk3.at[1], chunk3.at[2]))]
        for chunk in chunks:
            chunk.start()
        for g in (1, 0, 2):
            chunks[g].wait()
            for src in range(8):
                lines = in_s[g, src].astype(F32).reshape(32, 1024)
                for kz in range(8):
                    d_s[kz, src * 96 + g * 32 : src * 96 + g * 32 + 32, :] = lines[:, kz * 128 : kz * 128 + 128]

        def fetch(row, k, b):
            return d_s[FINE * b + k, pl.ds(row, 8, stride=96), :]

        def line(n, m):
            return lax.shift_right_logical(n, 3) * 32 + m * 8 + lax.bitwise_and(n, 7)

        def put_w(i, row_of):
            for kx, k, tiles in PARTS:
                for b in range(WIDE):
                    w_s[i, tiles.start + b] = fetch(row_of(kx), k, b)

        def fill(n, carry):
            put_w(n, lambda kx: line(n, kx))
            return carry

        lax.fori_loop(0, 24, fill, 0)

        def begin(n, carry):
            w = load(w_s, n)
            keep = rowmask[n]
            for kx, k, tiles in PARTS:
                diff = jnp.stack([fetch(line(n, 2 + kx), k, b) for b in range(WIDE)])
                xb, xa = x_pair(w, kx, k, masks)
                zb, za = z_pair(w, kx, k, masks)
                ys = w_s[n + 1, tiles] - w_s[n - 1, tiles]
                for c, s in enumerate(((xa - xb) * 0.5, ys * 0.5, (za - zb) * 0.5)):
                    im = keep / (s * s + (stencil_diag * smoothing + damping))
                    s_s[c, n, tiles] = s
                    im_s[c, n, tiles] = im
                    v0[c, n, tiles] = -s * diff * im
            return carry

        for c in range(3):
            for n in (0, 23):
                v0[c, n] = jnp.zeros((16, 8, 128), F32)
        lax.fori_loop(1, 23, begin, 0)

        for e, (edge, step) in enumerate(((0, 2), (23, -2))):
            w = load(w_s, edge)
            for kx, k, tiles in PARTS:
                lines = slice(tiles.start * 8, tiles.stop * 8)
                diff = jnp.stack([fetch(line(edge, 2 + kx), k, b) for b in range(WIDE)])
                xb, xa = x_pair(w, kx, k, masks)
                zb, za = z_pair(w, kx, k, masks)
                for slot, c, s in ((0, 0, (xa - xb) * 0.5), (1, 2, (za - zb) * 0.5)):
                    start = -s * diff / (s * s + (stencil_diag * smoothing + damping))
                    value = chain(c, tiles, edge + 4 * step, step) * start * rowmask[edge]
                    ends[e, slot, lines, :] = value.reshape(WIDE * 8, 128)
                ends[e, 2, lines, :] = (chain(1, tiles, edge + 4 * step, step) * rowmask[edge]).reshape(WIDE * 8, 128)
                ends[e, 3, lines, :] = w_s[edge + step // 2, tiles].reshape(WIDE * 8, 128)
                ends[e, 4, lines, :] = diff.reshape(WIDE * 8, 128)

    def iterate(u_s, v3, v4):
        vs = [v0, v1, v2, v3, v4]

        def copy(j):
            return pltpu.make_async_copy(vs[j].at[:, pl.ds(8 - 2 * j, 8)], vout.at[j], sems.at[j])

        s_copy = pltpu.make_async_copy(s_s.at[:, pl.ds(8, 8)], sout, sems.at[5])
        s_copy.start()
        copy(0).start()

        for j in range(4):
            gain = (1.0 if j == 0 else 2.0) / HALF
            old, new = vs[j], vs[j + 1]
            off = 2 * j

            def first(n, carry):
                scale = rowmask[n] * (gain * smoothing)
                for c in range(3):
                    v = load(old, c, n - off)
                    for kx, k, tiles in PARTS:
                        total = beside(v, kx, k, masks) + (old[c, n - off - 1, tiles] + old[c, n - off + 1, tiles])
                        u_s[c, n - 1, tiles] = (6.0 * v[kx, k] - total) * scale
                return carry

            lax.fori_loop(off + 1, 23 - off, first, 0)

            def second(n, carry):
                dots = {}
                for kx, k, tiles in PARTS:
                    dot = s_s[0, n, tiles] * old[0, n - off, tiles]
                    dot = dot + s_s[1, n, tiles] * old[1, n - off, tiles]
                    dots[kx, k] = (dot + s_s[2, n, tiles] * old[2, n - off, tiles]) * gain
                for c in range(3):
                    u = load(u_s, c, n - 1)
                    for kx, k, tiles in PARTS:
                        total = beside(u, kx, k, masks) + (u_s[c, n - 2, tiles] + u_s[c, n, tiles])
                        v = old[c, n - off, tiles]
                        image = s_s[c, n, tiles] * dots[kx, k] + (6.0 * u[kx, k] - total) + (gain * damping) * v
                        value = im_s[c, n, tiles] * image - (gain * CENTRE) * v
                        if j > 0:
                            value = value - vs[j - 1][c, n - off + 2, tiles]
                        new[c, n - off - 2, tiles] = value
                return carry

            lax.fori_loop(off + 2, 22 - off, second, 0)
            copy(j + 1).start()

        def products(n, sums):
            sums = list(sums)
            for c in range(3):
                for kx, k, tiles in PARTS:
                    s = s_s[c, n, tiles]
                    m = s * s + (stencil_diag * smoothing + damping)
                    v = [vs[j][c, n - 2 * j, tiles] for j in range(5)]
                    for j in range(4):
                        t = m * v[j]
                        for q, other in ((2 * j, v[j]), (2 * j + 1, v[j + 1])):
                            sums[q] = sums[q] + jnp.sum(t * other, axis=0)
            return tuple(sums)

        sums = list(lax.fori_loop(8, 16, products, tuple(jnp.zeros((8, 128), F32) for _ in range(8))))
        for first_row, step in ((8, 2), (15, -2)):
            end = first_row + 4 * step
            for c in range(3):
                for kx, k, tiles in PARTS:
                    share = chain(c, tiles, end, step) * v0[c, first_row, tiles]
                    s = s_s[c, end, tiles]
                    m = s * s + (stencil_diag * smoothing + damping)
                    sums[7] = sums[7] + jnp.sum(m * share * v3[c, end - 6, tiles], axis=0)
        lane = lax.broadcasted_iota(jnp.int32, (1, 128), 1)
        out = jnp.zeros((1, 128), F32)
        for q in range(8):
            out = jnp.where(lane == q, jnp.sum(sums[q], keepdims=True), out)
        mom[...] = jnp.broadcast_to(out, mom.shape)
        s_copy.wait()
        for j in range(5):
            copy(j).wait()

    pl.run_scoped(
        prepare,
        pltpu.VMEM((3, 8, 4, 8, 1024), BF16),
        pltpu.VMEM((8, 768, 128), F32),
        pltpu.VMEM((24, 16, 8, 128), F32),
        pltpu.SemaphoreType.DMA((3,)),
    )
    pl.run_scoped(iterate, field(22), field(12), field(8))


def krylov(chunks, rowmask, peers):
    vmem = pl.BlockSpec(memory_space=pltpu.VMEM)
    hbm = pl.BlockSpec(memory_space=pltpu.HBM)

    return pl.pallas_call(
        krylov_kernel,
        out_shape=(
            jax.ShapeDtypeStruct((peers, 128), F32),
            jax.ShapeDtypeStruct((5, 3, 8, 16, 8, 128), F32),
            jax.ShapeDtypeStruct((3, 8, 16, 8, 128), F32),
            jax.ShapeDtypeStruct((2, 5, 128, 128), F32),
        ),
        in_specs=[pl.BlockSpec(memory_space=pltpu.SMEM)] + [hbm],
        out_specs=(vmem, hbm, hbm, vmem),
        scratch_shapes=[
            field(24),
            field(24),
            field(24),
            field(20),
            field(16),
            pltpu.SemaphoreType.DMA((6,)),
        ],
        compiler_params=pltpu.CompilerParams(vmem_limit_bytes=31 * 1024 * 1024),
        cost_estimate=pl.CostEstimate(flops=400_000_000, bytes_accessed=60_000_000, transcendentals=0),
        name="krylov",
    )(rowmask, *chunks)


def ends_kernel(ends, far0, far1, out, rows):
    for e, far in enumerate((far0, far1)):
        lines = far[...].astype(F32).reshape(16, 1024)
        for kz in range(8):
            rows[kz] = lines[:, kz * 128 : kz * 128 + 128]
        for slot, c in ((0, 0), (1, 2)):
            out[e, c] = ends[e, slot]
        for kx, k, tiles in PARTS:
            for b in range(WIDE):
                at = slice((tiles.start + b) * 8, (tiles.start + b) * 8 + 8)
                beyond = rows[FINE * b + k, pl.ds(kx, 8, stride=2), :]
                near = ends[e, 3, at, :]
                s = (near - beyond) * 0.5 if e == 0 else (beyond - near) * 0.5
                start = -s * ends[e, 4, at, :] / (s * s + (stencil_diag * smoothing + damping))
                out[e, 1, at, :] = ends[e, 2, at, :] * start


def outer_rows(ends, far0, far1):
    vmem = pl.BlockSpec(memory_space=pltpu.VMEM)
    return pl.pallas_call(
        ends_kernel,
        out_shape=jax.ShapeDtypeStruct((2, 3, 128, 128), F32),
        in_specs=[vmem] * 3,
        out_specs=vmem,
        scratch_shapes=[pltpu.VMEM((8, 16, 128), F32)],
        compiler_params=pltpu.CompilerParams(vmem_limit_bytes=4 * 1024 * 1024),
        name="outer_rows",
    )(ends, far0, far1)


def coefficients(m):
    def lam(k):
        if k == 0:
            return CENTRE * m[0] + HALF * m[1]
        return CENTRE * m[k] + (HALF / 2) * (m[k + 1] + m[k - 1])

    lams = [lam(k) for k in range(7)]
    rows = [[0.5 * (lams[i + j] + lams[abs(i - j)]) for j in range(4)] + [m[i]] for i in range(4)]
    for p in range(4):
        inverse = 1.0 / rows[p][p]
        for q in range(p + 1, 4):
            factor = rows[q][p] * inverse
            rows[q] = [rows[q][k] - factor * rows[p][k] if k > p else rows[q][k] for k in range(5)]
    part = [None] * 4
    for p in reversed(range(4)):
        value = rows[p][4]
        for q in range(p + 1, 4):
            value = value - rows[p][q] * part[q]
        part[p] = value / rows[p][p]
    rest = [1.0 - CENTRE * part[0] - (HALF / 2) * part[1]]
    rest.append(-CENTRE * part[1] - HALF * part[0] - (HALF / 2) * part[2])
    rest.append(-CENTRE * part[2] - (HALF / 2) * (part[1] + part[3]))
    rest.append(-CENTRE * part[3] - (HALF / 2) * part[2])
    rest.append(-(HALF / 2) * part[3])
    return part, rest


def combine_kernel(mom, v_hbm, s_hbm, outer, out, v, s, turn, sems):
    loads = []
    for c in range(3):
        loads.append((
            pltpu.make_async_copy(v_hbm.at[:, c], v.at[:, c], sems.at[0, c]),
            pltpu.make_async_copy(s_hbm.at[c], s.at[c], sems.at[1, c]),
        ))
    for pair in loads:
        for each in pair:
            each.start()
    line = jnp.sum(mom[...], axis=0, keepdims=True)
    lane = lax.broadcasted_iota(jnp.int32, (1, 128), 1)
    p = [jnp.sum(jnp.where(lane == k, line, 0.0), axis=1, keepdims=True) for k in range(8)]
    m = [p[0], p[1]] + [2.0 * p[k] - p[k % 2] for k in range(2, 8)]
    part, rest = coefficients(m)
    part = [jnp.broadcast_to(x, (8, 128)) for x in part]
    rest = [jnp.broadcast_to(x, (8, 128)) for x in rest]

    for c in range(3):
        for each in loads[c]:
            each.wait()

        def row(i, carry):
            for kx, k, tiles in PARTS:
                at = pl.ds(pl.multiple_of((kx * 8 + i) * 8, 8), 8)
                for b in range(WIDE):
                    vecs = [v[j, c, i, tiles.start + b] for j in range(5)]
                    slope = s[c, i, tiles.start + b]
                    weight = slope * slope + (stencil_diag * smoothing + damping)
                    turn[c, 0, FINE * b + k, at, :] = sum(part[j] * vecs[j] for j in range(4))
                    turn[c, 1, FINE * b + k, at, :] = weight * sum(rest[j] * vecs[j] for j in range(5))
            return carry

        lax.fori_loop(0, 8, row, 0)
        for e, i in ((0, 0), (1, 7)):
            for kx, k, tiles in PARTS:
                at = slice((kx * 8 + i) * 8, (kx * 8 + i) * 8 + 8)
                for b in range(WIDE):
                    m = tiles.start + b
                    slope = s[c, i, m]
                    weight = slope * slope + (stencil_diag * smoothing + damping)
                    turn[c, 1, FINE * b + k, at, :] += weight * rest[4] * outer[e, c, m * 8 : m * 8 + 8, :]
        for q in range(2):
            for dest in range(8):
                for kz in range(8):
                    lanes = slice(kz * 128, kz * 128 + 128)
                    out[dest, q, c, :, lanes] = turn[c, q, kz, pl.ds(dest, 16, stride=8), :].astype(BF16)


def combine(moments, vectors, slopes, outer):
    vmem = pl.BlockSpec(memory_space=pltpu.VMEM)
    hbm = pl.BlockSpec(memory_space=pltpu.HBM)
    return pl.pallas_call(
        combine_kernel,
        out_shape=jax.ShapeDtypeStruct((8, 2, 3, 16, 1024), BF16),
        in_specs=[vmem, hbm, hbm, vmem],
        out_specs=vmem,
        scratch_shapes=[
            pltpu.VMEM(vectors.shape, F32),
            pltpu.VMEM(slopes.shape, F32),
            pltpu.VMEM((3, 2, 8, 128, 128), F32),
            pltpu.SemaphoreType.DMA((2, 3)),
        ],
        compiler_params=pltpu.CompilerParams(vmem_limit_bytes=24 * 1024 * 1024),
        name="combine",
    )(moments, vectors, slopes, outer)


def finish_kernel(flip, back, perm, sol, res):
    lines = jnp.concatenate([back[src, q, 0] for q in range(2) for src in range(8)], axis=0)
    lines = jnp.concatenate([lines[:, b * SPAN : b * SPAN + SPAN] for b in range(WIDE)], axis=0)
    cells = lax.dot_general(lines, perm[...], (((1,), (1,)), ((), ())), preferred_element_type=F32)
    for b in range(WIDE):
        for q, out in ((0, sol), (1, res)):
            for src in range(8):
                rows = pl.ds(pl.multiple_of((src + flip[0] * (7 - 2 * src)) * 8, 8), 8)
                for kx in range(2):
                    at = b * 256 + q * 128 + src * 16 + kx * 8
                    out[0, kx, rows, b * SPAN : b * SPAN + SPAN] = cells[at : at + 8]


def finish(back, flip, perm):
    shape = jax.ShapeDtypeStruct((3, 2, 64, 1024), F32)
    spec = pl.BlockSpec((1, 2, 64, 1024), lambda c: (c, 0, 0, 0))
    return pl.pallas_call(
        finish_kernel,
        grid=(3,),
        out_shape=(shape, shape),
        in_specs=[
            pl.BlockSpec(memory_space=pltpu.SMEM),
            pl.BlockSpec((8, 2, 1, 16, 1024), lambda c: (0, 0, c, 0, 0)),
            pl.BlockSpec((SPAN, SPAN), lambda c: (0, 0)),
        ],
        out_specs=(spec, spec),
        compiler_params=pltpu.CompilerParams(vmem_limit_bytes=14 * 1024 * 1024),
        name="finish",
    )(flip, back, perm)


def ring(cells, step):
    slabs, rows = lax.axis_size("slab"), lax.axis_size("row")

    def device(chunk):
        row, place = chunk // slabs, chunk % slabs
        return (place if row % 2 == 0 else slabs - 1 - place) * rows + row

    chunks = range(max(0, -step), slabs * rows - max(0, step))
    return lax.ppermute(cells, BOTH, [(device(i), device(i + step)) for i in chunks])


def per_device(moving, fixed, requests, footpoints, offset_x, offset_y, offset_z, fractions):
    depth, height, width = moving.shape
    perm = spread()
    block, slab = lax.axis_index("row"), lax.axis_index("slab")
    flip = block % 2
    start = block * height + (slab + flip * (7 - 2 * slab)) * 8 - 8
    peers, slots = requests.shape[2:]
    asked = jnp.pad(requests[0, 0], ((0, 0), (0, 128 - slots)))
    asked = lax.all_to_all(asked, BOTH, split_axis=0, concat_axis=0, tiled=True)
    outgoing = pick(asked, moving, slots)
    arrived = lax.all_to_all(outgoing, BOTH, split_axis=0, concat_axis=0, tiled=True)
    arrived = arrived.reshape(peers * slots, depth * TY, TZ)
    flip = flip.reshape(1)
    own = warp(
        arrived, footpoints[0, 0], offset_x[0, 0], offset_y[0, 0], offset_z[0, 0], fractions[0, 0], flip, fixed, perm
    )
    own = lax.all_to_all(own, "slab", split_axis=0, concat_axis=0, tiled=True)
    chunks = (jnp.stack([ring(own, 1), own, ring(own, -1)]),)
    rows = start + jnp.arange(24, dtype=jnp.int32)
    rowmask = ((rows >= 0) & (rows < height * lax.axis_size("row"))).astype(F32)
    moments, vectors, slopes, ends = krylov(chunks, rowmask, peers)
    far = (ring(own[:, 0:2, 7], 2), ring(own[:, 0:2, 0], -2))
    moments, far = lax.optimization_barrier((moments, far))
    outer = outer_rows(ends, *far)
    moments, outer = lax.optimization_barrier((moments, outer))
    moments = lax.all_to_all(moments, BOTH, split_axis=0, concat_axis=0, tiled=True)
    back = combine(moments, vectors, slopes, outer)
    back = lax.all_to_all(back, "slab", split_axis=0, concat_axis=0, tiled=True)
    return finish(back, flip, perm)


def solution(mesh):
    return jax.shard_map(
        per_device,
        mesh=mesh,
        in_specs=(
            P("slab", "row", None),
            P("slab", "row", None),
            P("slab", "row", None, None),
            P("slab", "row", None, None),
            P("slab", "row", None),
            P("slab", "row", None),
            P("slab", "row", None),
            P("slab", "row", None, None),
        ),
        out_specs=(P(None, "slab", "row", None), P(None, "slab", "row", None)),
        check_vma=False,
    )
```

```python
import functools

import jax
import jax.numpy as jnp
from jax import lax
from jax.experimental import pallas as pl
from jax.experimental.pallas import tpu as pltpu
from jax.sharding import PartitionSpec as P

TY = 16
TZ = 128
ITERS = 4

smoothing = 0.02
damping = 0.1
stencil_diag = 42.0

LOW = 0.1
HIGH = 3.2
CENTRE = (HIGH + LOW) / 2
HALF = (HIGH - LOW) / 2
REACH = (smoothing / HALF) ** 4 * 8

FINE = 4
WIDE = 8 // FINE
SPAN = 128 * FINE

BOTH = ("slab", "row")
F32 = jnp.float32
BF16 = jnp.bfloat16


def spread():
    source = lax.broadcasted_iota(jnp.int32, (SPAN, SPAN), 0)
    target = lax.broadcasted_iota(jnp.int32, (SPAN, SPAN), 1)
    return (target == (source % FINE) * 128 + source // FINE).astype(BF16)


def pick_kernel(asked_hbm, moving, out, asked, block, buf, loads, stores):
    peers, slots, depth = buf.shape[:3]
    count = stores.shape[0]
    first = pltpu.make_async_copy(asked_hbm, asked, loads.at[0])
    second = pltpu.make_async_copy(moving, block, loads.at[1])
    first.start()
    second.start()
    first.wait()
    second.wait()

    def peer(p, carry):
        for slot in range(slots):
            number = asked[p, slot]
            tile = jnp.maximum(number, 0)
            rows = pl.ds(pl.multiple_of(lax.shift_right_logical(tile, 3) * TY, TY), TY)
            lanes = pl.ds(pl.multiple_of(lax.bitwise_and(tile, 7) * TZ, TZ), TZ)
            for x in range(depth):
                cells = block[x, rows, lanes]
                buf[p, slot, x] = jnp.where(number >= 0, cells, jnp.zeros_like(cells))
        return carry

    part = peers // count
    sent = []
    for i in range(count):
        lax.fori_loop(i * part, (i + 1) * part, peer, 0, unroll=8)
        mine = pl.ds(i * part, part)
        sent.append(pltpu.make_async_copy(buf.at[mine], out.at[mine], stores.at[i]))
        sent[-1].start()
    for each in sent:
        each.wait()


def pick(asked, moving, slots):
    hbm = pl.BlockSpec(memory_space=pltpu.HBM)
    shape = (asked.shape[0], slots, moving.shape[0], TY, TZ)
    return pl.pallas_call(
        pick_kernel,
        out_shape=jax.ShapeDtypeStruct(shape, BF16),
        in_specs=[hbm, hbm],
        out_specs=hbm,
        scratch_shapes=[
            pltpu.SMEM(asked.shape, jnp.int32),
            pltpu.VMEM(moving.shape, BF16),
            pltpu.VMEM(shape, BF16),
            pltpu.SemaphoreType.DMA((2,)),
            pltpu.SemaphoreType.DMA((4,)),
        ],
        compiler_params=pltpu.CompilerParams(vmem_limit_bytes=62 * 1024 * 1024),
        name="pick",
    )(asked, moving)


def warp_kernel(foot, ox, oy, oz, wts, flip, arrived, fixed, perm, out, nat):
    base_z = lax.broadcasted_iota(jnp.int32, (256, 128), 0) - lax.broadcasted_iota(jnp.int32, (256, 128), 1)
    ro = lax.broadcasted_iota(jnp.int32, (64, 128), 0)
    ci = lax.broadcasted_iota(jnp.int32, (64, 128), 1)
    same = (ro // 32 == ci // 64) & ((ro // 16) % 2 == (ci // 16) % 2)
    base_y = jnp.where(same, ((ci // 32) % 2) * 16 + ci % 16 - ro % 16, -1000)

    def band(base, shift, here, after):
        return jnp.where(base == shift, here, jnp.where(base == shift + 1, after, 0.0)).astype(BF16)

    def tile_row(j, carry):
        rows = pl.ds(pl.multiple_of(j * 16, 16), 16)
        firsts = []
        for k in range(8):
            t = j * 8 + k
            sides = []
            for c in range(2):
                corners = [arrived[foot[t * 8 + 4 * a + 2 * b + c]] for a in range(2) for b in range(2)]
                sides.append(jnp.concatenate(corners, axis=0))
            wz = band(base_z, oz[t], wts[t * 6 + 4], wts[t * 6 + 5])
            firsts.append(jnp.dot(jnp.concatenate(sides, axis=1), wz, preferred_element_type=F32).astype(BF16))
        seconds = []
        for k in range(8):
            t = j * 8 + k
            wy = band(base_y, oy[t], wts[t * 6 + 2], wts[t * 6 + 3])
            seconds.append(jnp.dot(wy, firsts[k], preferred_element_type=F32).astype(BF16).astype(F32))
        for k in range(8):
            t = j * 8 + k
            shift = ox[t]
            lanes = slice(k * 128, (k + 1) * 128)
            for xo in range(2):
                total = None
                for p in range(xo, xo + 3):
                    weight = jnp.where(
                        p - xo == shift, wts[t * 6], jnp.where(p - xo == shift + 1, wts[t * 6 + 1], 0.0)
                    )
                    term = weight * seconds[k][p * 16 : (p + 1) * 16]
                    total = term if total is None else total + term
                nat[xo, rows, lanes] = total.astype(BF16)
                nat[2 + xo, rows, lanes] = (total - fixed[xo, rows, lanes]).astype(BF16)
        return carry

    lax.fori_loop(0, 4, tile_row, 0)
    for b in range(WIDE):
        lanes = slice(b * SPAN, b * SPAN + SPAN)
        mixed = jnp.dot(nat[:, :, lanes].reshape(256, SPAN), perm[...], preferred_element_type=F32)
        for place in range(8):
            dest = place + flip[0] * (7 - 2 * place)
            for m in range(4):
                out[dest, m, :, lanes] = mixed[m * 64 + place * 8 : m * 64 + place * 8 + 8].astype(BF16)


def warp(arrived, footpoints, offset_x, offset_y, offset_z, fractions, flip, fixed, perm):
    near = lax.reduce_precision(1.0 - fractions, 8, 7)
    far = lax.reduce_precision(fractions, 8, 7)
    wts = jnp.stack([near, far], axis=-1).reshape(-1)
    smem = pl.BlockSpec(memory_space=pltpu.SMEM)
    vmem = pl.BlockSpec(memory_space=pltpu.VMEM)
    return pl.pallas_call(
        warp_kernel,
        out_shape=jax.ShapeDtypeStruct((8, 4, 8, 1024), BF16),
        in_specs=[smem] * 6 + [vmem] * 3,
        out_specs=vmem,
        scratch_shapes=[pltpu.VMEM((4, 64, 1024), BF16)],
        compiler_params=pltpu.CompilerParams(vmem_limit_bytes=10 * 1024 * 1024),
        name="warp",
    )(footpoints.reshape(-1), offset_x, offset_y, offset_z, wts, flip, arrived, fixed, perm)


PARTS = [
    (kx, k, slice(kx * 8 + k * WIDE, kx * 8 + k * WIDE + WIDE)) for kx in range(2) for k in range(FINE)
]


def edge_masks():
    sub = lax.broadcasted_iota(jnp.int32, (1, 8, 128), 1)
    lane = lax.broadcasted_iota(jnp.int32, (WIDE, 8, 128), 2)
    one = lambda flag: jnp.where(flag, 1.0, 0.0).astype(F32)
    return one(sub != 0), one(sub != 7), lane == 0, lane == 127


def load(ref, *at):
    return {(kx, k): ref[(*at, tiles)] for kx, k, tiles in PARTS}


def x_pair(v, kx, k, masks):
    other = v[1 - kx, k]
    if kx == 0:
        return pltpu.roll(other, 1, 1) * masks[0], other
    return other, pltpu.roll(other, 7, 1) * masks[1]


def z_pair(v, kx, k, masks):
    nothing = jnp.zeros((1, 8, 128), F32)
    if k > 0:
        before = v[kx, k - 1]
    else:
        turned = pltpu.roll(v[kx, FINE - 1], 1, 2)
        carried = jnp.concatenate([nothing, turned[: WIDE - 1]], axis=0) if WIDE > 1 else nothing
        before = jnp.where(masks[2], carried, turned)
    if k < FINE - 1:
        after = v[kx, k + 1]
    else:
        turned = pltpu.roll(v[kx, 0], 127, 2)
        carried = jnp.concatenate([turned[1:], nothing], axis=0) if WIDE > 1 else nothing
        after = jnp.where(masks[3], carried, turned)
    return before, after


def beside(v, kx, k, masks):
    x0, x1 = x_pair(v, kx, k, masks)
    z0, z1 = z_pair(v, kx, k, masks)
    return (x0 + x1) + (z0 + z1)


def field(rows):
    return pltpu.VMEM((3, rows, 16, 8, 128), F32)


def krylov_kernel(rowmask, chunk3, mom, vout, sout, ends, s_s, im_s, v0, v1, v2, sems):
    masks = edge_masks()

    def chain(c, tiles, end, step):
        one = im_s[c, end, tiles] * im_s[c, end - step, tiles]
        return one * (im_s[c, end - 2 * step, tiles] * im_s[c, end - 3 * step, tiles]) * REACH

    def prepare(in_s, d_s, w_s, in_sems):
        chunks = [pltpu.make_async_copy(ref, in_s.at[g], in_sems.at[g]) for g, ref in enumerate((chunk3.at[0], chunk3.at[1], chunk3.at[2]))]
        for chunk in chunks:
            chunk.start()
        for g in (1, 0, 2):
            chunks[g].wait()
            for src in range(8):
                lines = in_s[g, src].astype(F32).reshape(32, 1024)
                for kz in range(8):
                    d_s[kz, src * 96 + g * 32 : src * 96 + g * 32 + 32, :] = lines[:, kz * 128 : kz * 128 + 128]

        def fetch(row, k, b):
            return d_s[FINE * b + k, pl.ds(row, 8, stride=96), :]

        def line(n, m):
            return lax.shift_right_logical(n, 3) * 32 + m * 8 + lax.bitwise_and(n, 7)

        def put_w(i, row_of):
            for kx, k, tiles in PARTS:
                for b in range(WIDE):
                    w_s[i, tiles.start + b] = fetch(row_of(kx), k, b)

        def fill(n, carry):
            put_w(n, lambda kx: line(n, kx))
            return carry

        lax.fori_loop(0, 24, fill, 0, unroll=4)

        def begin(n, carry):
            w = load(w_s, n)
            keep = rowmask[n]
            for kx, k, tiles in PARTS:
                diff = jnp.stack([fetch(line(n, 2 + kx), k, b) for b in range(WIDE)])
                xb, xa = x_pair(w, kx, k, masks)
                zb, za = z_pair(w, kx, k, masks)
                ys = w_s[n + 1, tiles] - w_s[n - 1, tiles]
                for c, s in enumerate(((xa - xb) * 0.5, ys * 0.5, (za - zb) * 0.5)):
                    im = keep / (s * s + (stencil_diag * smoothing + damping))
                    s_s[c, n, tiles] = s
                    im_s[c, n, tiles] = im
                    v0[c, n, tiles] = -s * diff * im
            return carry

        for c in range(3):
            for n in (0, 23):
                v0[c, n] = jnp.zeros((16, 8, 128), F32)
        lax.fori_loop(1, 23, begin, 0, unroll=2)

        for e, (edge, step) in enumerate(((0, 2), (23, -2))):
            w = load(w_s, edge)
            for kx, k, tiles in PARTS:
                lines = slice(tiles.start * 8, tiles.stop * 8)
                diff = jnp.stack([fetch(line(edge, 2 + kx), k, b) for b in range(WIDE)])
                xb, xa = x_pair(w, kx, k, masks)
                zb, za = z_pair(w, kx, k, masks)
                for slot, c, s in ((0, 0, (xa - xb) * 0.5), (1, 2, (za - zb) * 0.5)):
                    start = -s * diff / (s * s + (stencil_diag * smoothing + damping))
                    value = chain(c, tiles, edge + 4 * step, step) * start * rowmask[edge]
                    ends[e, slot, lines, :] = value.reshape(WIDE * 8, 128)
                ends[e, 2, lines, :] = (chain(1, tiles, edge + 4 * step, step) * rowmask[edge]).reshape(WIDE * 8, 128)
                ends[e, 3, lines, :] = w_s[edge + step // 2, tiles].reshape(WIDE * 8, 128)
                ends[e, 4, lines, :] = diff.reshape(WIDE * 8, 128)

    def iterate(u_s, v3, v4):
        vs = [v0, v1, v2, v3, v4]

        def copy(j):
            return pltpu.make_async_copy(vs[j].at[:, pl.ds(8 - 2 * j, 8)], vout.at[j], sems.at[j])

        s_copy = pltpu.make_async_copy(s_s.at[:, pl.ds(8, 8)], sout, sems.at[5])
        s_copy.start()
        copy(0).start()

        for j in range(4):
            gain = (1.0 if j == 0 else 2.0) / HALF
            old, new = vs[j], vs[j + 1]
            off = 2 * j

            def first(n, carry):
                scale = rowmask[n] * (gain * smoothing)
                for c in range(3):
                    v = load(old, c, n - off)
                    for kx, k, tiles in PARTS:
                        total = beside(v, kx, k, masks) + (old[c, n - off - 1, tiles] + old[c, n - off + 1, tiles])
                        u_s[c, n - 1, tiles] = (6.0 * v[kx, k] - total) * scale
                return carry

            lax.fori_loop(off + 1, 23 - off, first, 0, unroll=2)

            def second(n, carry):
                dots = {}
                for kx, k, tiles in PARTS:
                    dot = s_s[0, n, tiles] * old[0, n - off, tiles]
                    dot = dot + s_s[1, n, tiles] * old[1, n - off, tiles]
                    dots[kx, k] = (dot + s_s[2, n, tiles] * old[2, n - off, tiles]) * gain
                for c in range(3):
                    u = load(u_s, c, n - 1)
                    for kx, k, tiles in PARTS:
                        total = beside(u, kx, k, masks) + (u_s[c, n - 2, tiles] + u_s[c, n, tiles])
                        v = old[c, n - off, tiles]
                        image = s_s[c, n, tiles] * dots[kx, k] + (6.0 * u[kx, k] - total) + (gain * damping) * v
                        value = im_s[c, n, tiles] * image - (gain * CENTRE) * v
                        if j > 0:
                            value = value - vs[j - 1][c, n - off + 2, tiles]
                        new[c, n - off - 2, tiles] = value
                return carry

            lax.fori_loop(off + 2, 22 - off, second, 0, unroll=2)
            copy(j + 1).start()

        def products(n, sums):
            sums = list(sums)
            for c in range(3):
                for kx, k, tiles in PARTS:
                    s = s_s[c, n, tiles]
                    m = s * s + (stencil_diag * smoothing + damping)
                    v = [vs[j][c, n - 2 * j, tiles] for j in range(5)]
                    for j in range(4):
                        t = m * v[j]
                        for q, other in ((2 * j, v[j]), (2 * j + 1, v[j + 1])):
                            sums[q] = sums[q] + jnp.sum(t * other, axis=0)
            return tuple(sums)

        sums = list(lax.fori_loop(8, 16, products, tuple(jnp.zeros((8, 128), F32) for _ in range(8)), unroll=2))
        for first_row, step in ((8, 2), (15, -2)):
            end = first_row + 4 * step
            for c in range(3):
                for kx, k, tiles in PARTS:
                    share = chain(c, tiles, end, step) * v0[c, first_row, tiles]
                    s = s_s[c, end, tiles]
                    m = s * s + (stencil_diag * smoothing + damping)
                    sums[7] = sums[7] + jnp.sum(m * share * v3[c, end - 6, tiles], axis=0)
        lane = lax.broadcasted_iota(jnp.int32, (1, 128), 1)
        out = jnp.zeros((1, 128), F32)
        for q in range(8):
            out = jnp.where(lane == q, jnp.sum(sums[q], keepdims=True), out)
        mom[...] = jnp.broadcast_to(out, mom.shape)
        s_copy.wait()
        for j in range(5):
            copy(j).wait()

    pl.run_scoped(
        prepare,
        pltpu.VMEM((3, 8, 4, 8, 1024), BF16),
        pltpu.VMEM((8, 768, 128), F32),
        pltpu.VMEM((24, 16, 8, 128), F32),
        pltpu.SemaphoreType.DMA((3,)),
    )
    pl.run_scoped(iterate, field(22), field(12), field(8))


def krylov(chunks, rowmask, peers):
    vmem = pl.BlockSpec(memory_space=pltpu.VMEM)
    hbm = pl.BlockSpec(memory_space=pltpu.HBM)

    return pl.pallas_call(
        krylov_kernel,
        out_shape=(
            jax.ShapeDtypeStruct((peers, 128), F32),
            jax.ShapeDtypeStruct((5, 3, 8, 16, 8, 128), F32),
            jax.ShapeDtypeStruct((3, 8, 16, 8, 128), F32),
            jax.ShapeDtypeStruct((2, 5, 128, 128), F32),
        ),
        in_specs=[pl.BlockSpec(memory_space=pltpu.SMEM)] + [hbm],
        out_specs=(vmem, hbm, hbm, vmem),
        scratch_shapes=[
            field(24),
            field(24),
            field(24),
            field(20),
            field(16),
            pltpu.SemaphoreType.DMA((6,)),
        ],
        compiler_params=pltpu.CompilerParams(vmem_limit_bytes=31 * 1024 * 1024),
        cost_estimate=pl.CostEstimate(flops=400_000_000, bytes_accessed=60_000_000, transcendentals=0),
        name="krylov",
    )(rowmask, *chunks)


def ends_kernel(ends, far0, far1, out, rows):
    for e, far in enumerate((far0, far1)):
        lines = far[...].astype(F32).reshape(16, 1024)
        for kz in range(8):
            rows[kz] = lines[:, kz * 128 : kz * 128 + 128]
        for slot, c in ((0, 0), (1, 2)):
            out[e, c] = ends[e, slot]
        for kx, k, tiles in PARTS:
            for b in range(WIDE):
                at = slice((tiles.start + b) * 8, (tiles.start + b) * 8 + 8)
                beyond = rows[FINE * b + k, pl.ds(kx, 8, stride=2), :]
                near = ends[e, 3, at, :]
                s = (near - beyond) * 0.5 if e == 0 else (beyond - near) * 0.5
                start = -s * ends[e, 4, at, :] / (s * s + (stencil_diag * smoothing + damping))
                out[e, 1, at, :] = ends[e, 2, at, :] * start


def outer_rows(ends, far0, far1):
    vmem = pl.BlockSpec(memory_space=pltpu.VMEM)
    return pl.pallas_call(
        ends_kernel,
        out_shape=jax.ShapeDtypeStruct((2, 3, 128, 128), F32),
        in_specs=[vmem] * 3,
        out_specs=vmem,
        scratch_shapes=[pltpu.VMEM((8, 16, 128), F32)],
        compiler_params=pltpu.CompilerParams(vmem_limit_bytes=4 * 1024 * 1024),
        name="outer_rows",
    )(ends, far0, far1)


def coefficients(m):
    def lam(k):
        if k == 0:
            return CENTRE * m[0] + HALF * m[1]
        return CENTRE * m[k] + (HALF / 2) * (m[k + 1] + m[k - 1])

    lams = [lam(k) for k in range(7)]
    rows = [[0.5 * (lams[i + j] + lams[abs(i - j)]) for j in range(4)] + [m[i]] for i in range(4)]
    for p in range(4):
        inverse = 1.0 / rows[p][p]
        for q in range(p + 1, 4):
            factor = rows[q][p] * inverse
            rows[q] = [rows[q][k] - factor * rows[p][k] if k > p else rows[q][k] for k in range(5)]
    part = [None] * 4
    for p in reversed(range(4)):
        value = rows[p][4]
        for q in range(p + 1, 4):
            value = value - rows[p][q] * part[q]
        part[p] = value / rows[p][p]
    rest = [1.0 - CENTRE * part[0] - (HALF / 2) * part[1]]
    rest.append(-CENTRE * part[1] - HALF * part[0] - (HALF / 2) * part[2])
    rest.append(-CENTRE * part[2] - (HALF / 2) * (part[1] + part[3]))
    rest.append(-CENTRE * part[3] - (HALF / 2) * part[2])
    rest.append(-(HALF / 2) * part[3])
    return part, rest


def combine_kernel(mom, v_hbm, s_hbm, outer, out, v, s, turn, sems):
    loads = []
    for c in range(3):
        loads.append((
            pltpu.make_async_copy(v_hbm.at[:, c], v.at[:, c], sems.at[0, c]),
            pltpu.make_async_copy(s_hbm.at[c], s.at[c], sems.at[1, c]),
        ))
    for pair in loads:
        for each in pair:
            each.start()
    line = jnp.sum(mom[...], axis=0, keepdims=True)
    lane = lax.broadcasted_iota(jnp.int32, (1, 128), 1)
    p = [jnp.sum(jnp.where(lane == k, line, 0.0), axis=1, keepdims=True) for k in range(8)]
    m = [p[0], p[1]] + [2.0 * p[k] - p[k % 2] for k in range(2, 8)]
    part, rest = coefficients(m)
    part = [jnp.broadcast_to(x, (8, 128)) for x in part]
    rest = [jnp.broadcast_to(x, (8, 128)) for x in rest]

    for c in range(3):
        for each in loads[c]:
            each.wait()

        def row(i, carry):
            for kx, k, tiles in PARTS:
                at = pl.ds(pl.multiple_of((kx * 8 + i) * 8, 8), 8)
                for b in range(WIDE):
                    vecs = [v[j, c, i, tiles.start + b] for j in range(5)]
                    slope = s[c, i, tiles.start + b]
                    weight = slope * slope + (stencil_diag * smoothing + damping)
                    turn[c, 0, FINE * b + k, at, :] = sum(part[j] * vecs[j] for j in range(4))
                    turn[c, 1, FINE * b + k, at, :] = weight * sum(rest[j] * vecs[j] for j in range(5))
            return carry

        lax.fori_loop(0, 8, row, 0)
        for e, i in ((0, 0), (1, 7)):
            for kx, k, tiles in PARTS:
                at = slice((kx * 8 + i) * 8, (kx * 8 + i) * 8 + 8)
                for b in range(WIDE):
                    m = tiles.start + b
                    slope = s[c, i, m]
                    weight = slope * slope + (stencil_diag * smoothing + damping)
                    turn[c, 1, FINE * b + k, at, :] += weight * rest[4] * outer[e, c, m * 8 : m * 8 + 8, :]
        for q in range(2):
            for dest in range(8):
                for kz in range(8):
                    lanes = slice(kz * 128, kz * 128 + 128)
                    out[dest, q, c, :, lanes] = turn[c, q, kz, pl.ds(dest, 16, stride=8), :].astype(BF16)


def combine(moments, vectors, slopes, outer):
    vmem = pl.BlockSpec(memory_space=pltpu.VMEM)
    hbm = pl.BlockSpec(memory_space=pltpu.HBM)
    return pl.pallas_call(
        combine_kernel,
        out_shape=jax.ShapeDtypeStruct((8, 2, 3, 16, 1024), BF16),
        in_specs=[vmem, hbm, hbm, vmem],
        out_specs=vmem,
        scratch_shapes=[
            pltpu.VMEM(vectors.shape, F32),
            pltpu.VMEM(slopes.shape, F32),
            pltpu.VMEM((3, 2, 8, 128, 128), F32),
            pltpu.SemaphoreType.DMA((2, 3)),
        ],
        compiler_params=pltpu.CompilerParams(vmem_limit_bytes=24 * 1024 * 1024),
        name="combine",
    )(moments, vectors, slopes, outer)


def finish_kernel(flip, back, perm, sol, res):
    lines = jnp.concatenate([back[src, q, 0] for q in range(2) for src in range(8)], axis=0)
    lines = jnp.concatenate([lines[:, b * SPAN : b * SPAN + SPAN] for b in range(WIDE)], axis=0)
    cells = lax.dot_general(lines, perm[...], (((1,), (1,)), ((), ())), preferred_element_type=F32)
    for b in range(WIDE):
        for q, out in ((0, sol), (1, res)):
            for src in range(8):
                rows = pl.ds(pl.multiple_of((src + flip[0] * (7 - 2 * src)) * 8, 8), 8)
                for kx in range(2):
                    at = b * 256 + q * 128 + src * 16 + kx * 8
                    out[0, kx, rows, b * SPAN : b * SPAN + SPAN] = cells[at : at + 8]


def finish(back, flip, perm):
    shape = jax.ShapeDtypeStruct((3, 2, 64, 1024), F32)
    spec = pl.BlockSpec((1, 2, 64, 1024), lambda c: (c, 0, 0, 0))
    return pl.pallas_call(
        finish_kernel,
        grid=(3,),
        out_shape=(shape, shape),
        in_specs=[
            pl.BlockSpec(memory_space=pltpu.SMEM),
            pl.BlockSpec((8, 2, 1, 16, 1024), lambda c: (0, 0, c, 0, 0)),
            pl.BlockSpec((SPAN, SPAN), lambda c: (0, 0)),
        ],
        out_specs=(spec, spec),
        compiler_params=pltpu.CompilerParams(vmem_limit_bytes=14 * 1024 * 1024),
        name="finish",
    )(flip, back, perm)


def ring(cells, step):
    slabs, rows = lax.axis_size("slab"), lax.axis_size("row")

    def device(chunk):
        row, place = chunk // slabs, chunk % slabs
        return (place if row % 2 == 0 else slabs - 1 - place) * rows + row

    chunks = range(max(0, -step), slabs * rows - max(0, step))
    return lax.ppermute(cells, BOTH, [(device(i), device(i + step)) for i in chunks])


def per_device(moving, fixed, requests, footpoints, offset_x, offset_y, offset_z, fractions):
    depth, height, width = moving.shape
    perm = spread()
    block, slab = lax.axis_index("row"), lax.axis_index("slab")
    flip = block % 2
    start = block * height + (slab + flip * (7 - 2 * slab)) * 8 - 8
    peers, slots = requests.shape[2:]
    asked = jnp.pad(requests[0, 0], ((0, 0), (0, 128 - slots)))
    asked = lax.all_to_all(asked, BOTH, split_axis=0, concat_axis=0, tiled=True)
    outgoing = pick(asked, moving, slots)
    arrived = lax.all_to_all(outgoing, BOTH, split_axis=0, concat_axis=0, tiled=True)
    arrived = arrived.reshape(peers * slots, depth * TY, TZ)
    flip = flip.reshape(1)
    own = warp(
        arrived, footpoints[0, 0], offset_x[0, 0], offset_y[0, 0], offset_z[0, 0], fractions[0, 0], flip, fixed, perm
    )
    own = lax.all_to_all(own, "slab", split_axis=0, concat_axis=0, tiled=True)
    chunks = (jnp.stack([ring(own, 1), own, ring(own, -1)]),)
    rows = start + jnp.arange(24, dtype=jnp.int32)
    rowmask = ((rows >= 0) & (rows < height * lax.axis_size("row"))).astype(F32)
    moments, vectors, slopes, ends = krylov(chunks, rowmask, peers)
    far = (ring(own[:, 0:2, 7], 2), ring(own[:, 0:2, 0], -2))
    moments, far = lax.optimization_barrier((moments, far))
    outer = outer_rows(ends, *far)
    moments, outer = lax.optimization_barrier((moments, outer))
    moments = lax.all_to_all(moments, BOTH, split_axis=0, concat_axis=0, tiled=True)
    back = combine(moments, vectors, slopes, outer)
    back = lax.all_to_all(back, "slab", split_axis=0, concat_axis=0, tiled=True)
    return finish(back, flip, perm)


def solution(mesh):
    return jax.shard_map(
        per_device,
        mesh=mesh,
        in_specs=(
            P("slab", "row", None),
            P("slab", "row", None),
            P("slab", "row", None, None),
            P("slab", "row", None, None),
            P("slab", "row", None),
            P("slab", "row", None),
            P("slab", "row", None),
            P("slab", "row", None, None),
        ),
        out_specs=(P(None, "slab", "row", None), P(None, "slab", "row", None)),
        check_vma=False,
    )
```

```python
import functools

import jax
import jax.numpy as jnp
from jax import lax
from jax.experimental import pallas as pl
from jax.experimental.pallas import tpu as pltpu
from jax.sharding import PartitionSpec as P

TY = 16
TZ = 128
ITERS = 4

smoothing = 0.02
damping = 0.1
stencil_diag = 42.0

LOW = 0.1
HIGH = 3.2
CENTRE = (HIGH + LOW) / 2
HALF = (HIGH - LOW) / 2
REACH = (smoothing / HALF) ** 4 * 8

FINE = 4
WIDE = 8 // FINE
SPAN = 128 * FINE

BOTH = ("slab", "row")
F32 = jnp.float32
BF16 = jnp.bfloat16


def spread():
    source = lax.broadcasted_iota(jnp.int32, (SPAN, SPAN), 0)
    target = lax.broadcasted_iota(jnp.int32, (SPAN, SPAN), 1)
    return (target == (source % FINE) * 128 + source // FINE).astype(BF16)


def pick_kernel(asked_hbm, moving, out, asked, block, buf, loads, stores):
    peers, slots, depth = buf.shape[:3]
    count = stores.shape[0]
    first = pltpu.make_async_copy(asked_hbm, asked, loads.at[0])
    second = pltpu.make_async_copy(moving, block, loads.at[1])
    first.start()
    second.start()
    first.wait()
    second.wait()

    def peer(p, carry):
        for slot in range(slots):
            number = asked[p, slot]
            tile = jnp.maximum(number, 0)
            rows = pl.ds(pl.multiple_of(lax.shift_right_logical(tile, 3) * TY, TY), TY)
            lanes = pl.ds(pl.multiple_of(lax.bitwise_and(tile, 7) * TZ, TZ), TZ)
            for x in range(depth):
                cells = block[x, rows, lanes]
                buf[p, slot, x] = jnp.where(number >= 0, cells, jnp.zeros_like(cells))
        return carry

    part = peers // count
    sent = []
    for i in range(count):
        lax.fori_loop(i * part, (i + 1) * part, peer, 0, unroll=8)
        mine = pl.ds(i * part, part)
        sent.append(pltpu.make_async_copy(buf.at[mine], out.at[mine], stores.at[i]))
        sent[-1].start()
    for each in sent:
        each.wait()


def pick(asked, moving, slots):
    hbm = pl.BlockSpec(memory_space=pltpu.HBM)
    shape = (asked.shape[0], slots, moving.shape[0], TY, TZ)
    return pl.pallas_call(
        pick_kernel,
        out_shape=jax.ShapeDtypeStruct(shape, BF16),
        in_specs=[hbm, hbm],
        out_specs=hbm,
        scratch_shapes=[
            pltpu.SMEM(asked.shape, jnp.int32),
            pltpu.VMEM(moving.shape, BF16),
            pltpu.VMEM(shape, BF16),
            pltpu.SemaphoreType.DMA((2,)),
            pltpu.SemaphoreType.DMA((4,)),
        ],
        compiler_params=pltpu.CompilerParams(vmem_limit_bytes=62 * 1024 * 1024),
        name="pick",
    )(asked, moving)


def warp_kernel(foot, ox, oy, oz, wts, flip, arrived, fixed, perm, out, nat):
    base_z = lax.broadcasted_iota(jnp.int32, (256, 128), 0) - lax.broadcasted_iota(jnp.int32, (256, 128), 1)
    ro = lax.broadcasted_iota(jnp.int32, (64, 128), 0)
    ci = lax.broadcasted_iota(jnp.int32, (64, 128), 1)
    same = (ro // 32 == ci // 64) & ((ro // 16) % 2 == (ci // 16) % 2)
    base_y = jnp.where(same, ((ci // 32) % 2) * 16 + ci % 16 - ro % 16, -1000)

    def band(base, shift, here, after):
        return jnp.where(base == shift, here, jnp.where(base == shift + 1, after, 0.0)).astype(BF16)

    def tile_row(j, carry):
        rows = pl.ds(pl.multiple_of(j * 16, 16), 16)
        firsts = []
        for k in range(8):
            t = j * 8 + k
            sides = []
            for c in range(2):
                corners = [arrived[foot[t * 8 + 4 * a + 2 * b + c]] for a in range(2) for b in range(2)]
                sides.append(jnp.concatenate(corners, axis=0))
            wz = band(base_z, oz[t], wts[t * 6 + 4], wts[t * 6 + 5])
            firsts.append(jnp.dot(jnp.concatenate(sides, axis=1), wz, preferred_element_type=F32).astype(BF16))
        seconds = []
        for k in range(8):
            t = j * 8 + k
            wy = band(base_y, oy[t], wts[t * 6 + 2], wts[t * 6 + 3])
            seconds.append(jnp.dot(wy, firsts[k], preferred_element_type=F32).astype(BF16).astype(F32))
        for k in range(8):
            t = j * 8 + k
            shift = ox[t]
            lanes = slice(k * 128, (k + 1) * 128)
            for xo in range(2):
                total = None
                for p in range(xo, xo + 3):
                    weight = jnp.where(
                        p - xo == shift, wts[t * 6], jnp.where(p - xo == shift + 1, wts[t * 6 + 1], 0.0)
                    )
                    term = weight * seconds[k][p * 16 : (p + 1) * 16]
                    total = term if total is None else total + term
                nat[xo, rows, lanes] = total.astype(BF16)
                nat[2 + xo, rows, lanes] = (total - fixed[xo, rows, lanes]).astype(BF16)
        return carry

    lax.fori_loop(0, 4, tile_row, 0)
    for b in range(WIDE):
        lanes = slice(b * SPAN, b * SPAN + SPAN)
        mixed = jnp.dot(nat[:, :, lanes].reshape(256, SPAN), perm[...], preferred_element_type=F32)
        for place in range(8):
            dest = place + flip[0] * (7 - 2 * place)
            for m in range(4):
                out[dest, m, :, lanes] = mixed[m * 64 + place * 8 : m * 64 + place * 8 + 8].astype(BF16)


def warp(arrived, footpoints, offset_x, offset_y, offset_z, fractions, flip, fixed, perm):
    near = lax.reduce_precision(1.0 - fractions, 8, 7)
    far = lax.reduce_precision(fractions, 8, 7)
    wts = jnp.stack([near, far], axis=-1).reshape(-1)
    smem = pl.BlockSpec(memory_space=pltpu.SMEM)
    vmem = pl.BlockSpec(memory_space=pltpu.VMEM)
    return pl.pallas_call(
        warp_kernel,
        out_shape=jax.ShapeDtypeStruct((8, 4, 8, 1024), BF16),
        in_specs=[smem] * 6 + [vmem] * 3,
        out_specs=vmem,
        scratch_shapes=[pltpu.VMEM((4, 64, 1024), BF16)],
        compiler_params=pltpu.CompilerParams(vmem_limit_bytes=10 * 1024 * 1024),
        name="warp",
    )(footpoints.reshape(-1), offset_x, offset_y, offset_z, wts, flip, arrived, fixed, perm)


PARTS = [
    (kx, k, slice(kx * 8 + k * WIDE, kx * 8 + k * WIDE + WIDE)) for kx in range(2) for k in range(FINE)
]


def edge_masks():
    sub = lax.broadcasted_iota(jnp.int32, (1, 8, 128), 1)
    lane = lax.broadcasted_iota(jnp.int32, (WIDE, 8, 128), 2)
    one = lambda flag: jnp.where(flag, 1.0, 0.0).astype(F32)
    return one(sub != 0), one(sub != 7), lane == 0, lane == 127


def load(ref, *at):
    return {(kx, k): ref[(*at, tiles)] for kx, k, tiles in PARTS}


def x_pair(v, kx, k, masks):
    other = v[1 - kx, k]
    if kx == 0:
        return pltpu.roll(other, 1, 1) * masks[0], other
    return other, pltpu.roll(other, 7, 1) * masks[1]


def z_pair(v, kx, k, masks):
    nothing = jnp.zeros((1, 8, 128), F32)
    if k > 0:
        before = v[kx, k - 1]
    else:
        turned = pltpu.roll(v[kx, FINE - 1], 1, 2)
        carried = jnp.concatenate([nothing, turned[: WIDE - 1]], axis=0) if WIDE > 1 else nothing
        before = jnp.where(masks[2], carried, turned)
    if k < FINE - 1:
        after = v[kx, k + 1]
    else:
        turned = pltpu.roll(v[kx, 0], 127, 2)
        carried = jnp.concatenate([turned[1:], nothing], axis=0) if WIDE > 1 else nothing
        after = jnp.where(masks[3], carried, turned)
    return before, after


def beside(v, kx, k, masks):
    x0, x1 = x_pair(v, kx, k, masks)
    z0, z1 = z_pair(v, kx, k, masks)
    return (x0 + x1) + (z0 + z1)


def field(rows):
    return pltpu.VMEM((3, rows, 16, 8, 128), F32)


def krylov_kernel(place, rowmask, chunks, mom, vout, sout, ends, s_s, im_s, v0, v1, v2, sems):
    masks = edge_masks()

    def chain(c, tiles, end, step):
        one = im_s[c, end, tiles] * im_s[c, end - step, tiles]
        return one * (im_s[c, end - 2 * step, tiles] * im_s[c, end - 3 * step, tiles]) * REACH

    def prepare(in_s, d_s, w_s, in_sems):
        odd = lax.bitwise_and(place[0], 1)
        sources = (2 - 2 * odd, 1, 2 * odd)
        loads = [pltpu.make_async_copy(chunks.at[src], in_s.at[g], in_sems.at[g]) for g, src in enumerate(sources)]
        for each in loads:
            each.start()
        for g in (1, 0, 2):
            loads[g].wait()
            for src in range(8):
                lines = in_s[g, src].astype(F32).reshape(32, 1024)
                for kz in range(8):
                    d_s[kz, src * 96 + g * 32 : src * 96 + g * 32 + 32, :] = lines[:, kz * 128 : kz * 128 + 128]

        def fetch(row, k, b):
            return d_s[FINE * b + k, pl.ds(row, 8, stride=96), :]

        def line(n, m):
            return lax.shift_right_logical(n, 3) * 32 + m * 8 + lax.bitwise_and(n, 7)

        def put_w(i, row_of):
            for kx, k, tiles in PARTS:
                for b in range(WIDE):
                    w_s[i, tiles.start + b] = fetch(row_of(kx), k, b)

        def fill(n, carry):
            put_w(n, lambda kx: line(n, kx))
            return carry

        lax.fori_loop(0, 24, fill, 0, unroll=4)

        def begin(n, carry):
            w = load(w_s, n)
            keep = rowmask[n]
            for kx, k, tiles in PARTS:
                diff = jnp.stack([fetch(line(n, 2 + kx), k, b) for b in range(WIDE)])
                xb, xa = x_pair(w, kx, k, masks)
                zb, za = z_pair(w, kx, k, masks)
                ys = w_s[n + 1, tiles] - w_s[n - 1, tiles]
                for c, s in enumerate(((xa - xb) * 0.5, ys * 0.5, (za - zb) * 0.5)):
                    im = keep / (s * s + (stencil_diag * smoothing + damping))
                    s_s[c, n, tiles] = s
                    im_s[c, n, tiles] = im
                    v0[c, n, tiles] = -s * diff * im
            return carry

        for c in range(3):
            for n in (0, 23):
                v0[c, n] = jnp.zeros((16, 8, 128), F32)
        lax.fori_loop(1, 23, begin, 0, unroll=2)

        for e, (edge, step) in enumerate(((0, 2), (23, -2))):
            w = load(w_s, edge)
            for kx, k, tiles in PARTS:
                lines = slice(tiles.start * 8, tiles.stop * 8)
                diff = jnp.stack([fetch(line(edge, 2 + kx), k, b) for b in range(WIDE)])
                xb, xa = x_pair(w, kx, k, masks)
                zb, za = z_pair(w, kx, k, masks)
                for slot, c, s in ((0, 0, (xa - xb) * 0.5), (1, 2, (za - zb) * 0.5)):
                    start = -s * diff / (s * s + (stencil_diag * smoothing + damping))
                    value = chain(c, tiles, edge + 4 * step, step) * start * rowmask[edge]
                    ends[e, slot, lines, :] = value.reshape(WIDE * 8, 128)
                ends[e, 2, lines, :] = (chain(1, tiles, edge + 4 * step, step) * rowmask[edge]).reshape(WIDE * 8, 128)
                ends[e, 3, lines, :] = w_s[edge + step // 2, tiles].reshape(WIDE * 8, 128)
                ends[e, 4, lines, :] = diff.reshape(WIDE * 8, 128)

    def iterate(u_s, v3, v4):
        vs = [v0, v1, v2, v3, v4]

        def copy(j):
            return pltpu.make_async_copy(vs[j].at[:, pl.ds(8 - 2 * j, 8)], vout.at[j], sems.at[j])

        s_copy = pltpu.make_async_copy(s_s.at[:, pl.ds(8, 8)], sout, sems.at[5])
        s_copy.start()
        copy(0).start()

        for j in range(4):
            gain = (1.0 if j == 0 else 2.0) / HALF
            old, new = vs[j], vs[j + 1]
            off = 2 * j

            def first(n, carry):
                scale = rowmask[n] * (gain * smoothing)
                for c in range(3):
                    v = load(old, c, n - off)
                    for kx, k, tiles in PARTS:
                        total = beside(v, kx, k, masks) + (old[c, n - off - 1, tiles] + old[c, n - off + 1, tiles])
                        u_s[c, n - 1, tiles] = (6.0 * v[kx, k] - total) * scale
                return carry

            lax.fori_loop(off + 1, 23 - off, first, 0, unroll=2)

            def second(n, carry):
                dots = {}
                for kx, k, tiles in PARTS:
                    dot = s_s[0, n, tiles] * old[0, n - off, tiles]
                    dot = dot + s_s[1, n, tiles] * old[1, n - off, tiles]
                    dots[kx, k] = (dot + s_s[2, n, tiles] * old[2, n - off, tiles]) * gain
                for c in range(3):
                    u = load(u_s, c, n - 1)
                    for kx, k, tiles in PARTS:
                        total = beside(u, kx, k, masks) + (u_s[c, n - 2, tiles] + u_s[c, n, tiles])
                        v = old[c, n - off, tiles]
                        image = s_s[c, n, tiles] * dots[kx, k] + (6.0 * u[kx, k] - total) + (gain * damping) * v
                        value = im_s[c, n, tiles] * image - (gain * CENTRE) * v
                        if j > 0:
                            value = value - vs[j - 1][c, n - off + 2, tiles]
                        new[c, n - off - 2, tiles] = value
                return carry

            lax.fori_loop(off + 2, 22 - off, second, 0, unroll=2)
            copy(j + 1).start()

        def products(n, sums):
            sums = list(sums)
            for c in range(3):
                for kx, k, tiles in PARTS:
                    s = s_s[c, n, tiles]
                    m = s * s + (stencil_diag * smoothing + damping)
                    v = [vs[j][c, n - 2 * j, tiles] for j in range(5)]
                    for j in range(4):
                        t = m * v[j]
                        for q, other in ((2 * j, v[j]), (2 * j + 1, v[j + 1])):
                            sums[q] = sums[q] + jnp.sum(t * other, axis=0)
            return tuple(sums)

        sums = list(lax.fori_loop(8, 16, products, tuple(jnp.zeros((8, 128), F32) for _ in range(8)), unroll=2))
        for first_row, step in ((8, 2), (15, -2)):
            end = first_row + 4 * step
            for c in range(3):
                for kx, k, tiles in PARTS:
                    share = chain(c, tiles, end, step) * v0[c, first_row, tiles]
                    s = s_s[c, end, tiles]
                    m = s * s + (stencil_diag * smoothing + damping)
                    sums[7] = sums[7] + jnp.sum(m * share * v3[c, end - 6, tiles], axis=0)
        lane = lax.broadcasted_iota(jnp.int32, (1, 128), 1)
        out = jnp.zeros((1, 128), F32)
        for q in range(8):
            out = jnp.where(lane == q, jnp.sum(sums[q], keepdims=True), out)
        mom[...] = jnp.broadcast_to(out, mom.shape)
        s_copy.wait()
        for j in range(5):
            copy(j).wait()

    pl.run_scoped(
        prepare,
        pltpu.VMEM((3, 8, 4, 8, 1024), BF16),
        pltpu.VMEM((8, 768, 128), F32),
        pltpu.VMEM((24, 16, 8, 128), F32),
        pltpu.SemaphoreType.DMA((3,)),
    )
    pl.run_scoped(iterate, field(22), field(12), field(8))


def krylov(chunks, place, rowmask, peers):
    vmem = pl.BlockSpec(memory_space=pltpu.VMEM)
    hbm = pl.BlockSpec(memory_space=pltpu.HBM)

    return pl.pallas_call(
        krylov_kernel,
        out_shape=(
            jax.ShapeDtypeStruct((peers, 128), F32),
            jax.ShapeDtypeStruct((5, 3, 8, 16, 8, 128), F32),
            jax.ShapeDtypeStruct((3, 8, 16, 8, 128), F32),
            jax.ShapeDtypeStruct((2, 5, 128, 128), F32),
        ),
        in_specs=[pl.BlockSpec(memory_space=pltpu.SMEM)] * 2 + [hbm],
        out_specs=(vmem, hbm, hbm, vmem),
        scratch_shapes=[
            field(24),
            field(24),
            field(24),
            field(20),
            field(16),
            pltpu.SemaphoreType.DMA((6,)),
        ],
        compiler_params=pltpu.CompilerParams(vmem_limit_bytes=31 * 1024 * 1024),
        cost_estimate=pl.CostEstimate(flops=400_000_000, bytes_accessed=60_000_000, transcendentals=0),
        name="krylov",
    )(place, rowmask, chunks)


def ends_kernel(place, ends, inner, outer, out, rows):
    upper = lax.bitwise_and(place[0], 2) == 2
    both = [x[...].astype(F32).reshape(16, 1024) for x in (inner, outer)]
    for e in range(2):
        lines = jnp.where(upper, both[e], both[1 - e])
        for kz in range(8):
            rows[kz] = lines[:, kz * 128 : kz * 128 + 128]
        for slot, c in ((0, 0), (1, 2)):
            out[e, c] = ends[e, slot]
        for kx, k, tiles in PARTS:
            for b in range(WIDE):
                at = slice((tiles.start + b) * 8, (tiles.start + b) * 8 + 8)
                beyond = rows[FINE * b + k, pl.ds(kx, 8, stride=2), :]
                near = ends[e, 3, at, :]
                s = (near - beyond) * 0.5 if e == 0 else (beyond - near) * 0.5
                start = -s * ends[e, 4, at, :] / (s * s + (stencil_diag * smoothing + damping))
                out[e, 1, at, :] = ends[e, 2, at, :] * start


def outer_rows(ends, place, inner, outer):
    vmem = pl.BlockSpec(memory_space=pltpu.VMEM)
    return pl.pallas_call(
        ends_kernel,
        out_shape=jax.ShapeDtypeStruct((2, 3, 128, 128), F32),
        in_specs=[pl.BlockSpec(memory_space=pltpu.SMEM)] + [vmem] * 3,
        out_specs=vmem,
        scratch_shapes=[pltpu.VMEM((8, 16, 128), F32)],
        compiler_params=pltpu.CompilerParams(vmem_limit_bytes=4 * 1024 * 1024),
        name="outer_rows",
    )(place, ends, inner, outer)


def coefficients(m):
    def lam(k):
        if k == 0:
            return CENTRE * m[0] + HALF * m[1]
        return CENTRE * m[k] + (HALF / 2) * (m[k + 1] + m[k - 1])

    lams = [lam(k) for k in range(7)]
    rows = [[0.5 * (lams[i + j] + lams[abs(i - j)]) for j in range(4)] + [m[i]] for i in range(4)]
    for p in range(4):
        inverse = 1.0 / rows[p][p]
        for q in range(p + 1, 4):
            factor = rows[q][p] * inverse
            rows[q] = [rows[q][k] - factor * rows[p][k] if k > p else rows[q][k] for k in range(5)]
    part = [None] * 4
    for p in reversed(range(4)):
        value = rows[p][4]
        for q in range(p + 1, 4):
            value = value - rows[p][q] * part[q]
        part[p] = value / rows[p][p]
    rest = [1.0 - CENTRE * part[0] - (HALF / 2) * part[1]]
    rest.append(-CENTRE * part[1] - HALF * part[0] - (HALF / 2) * part[2])
    rest.append(-CENTRE * part[2] - (HALF / 2) * (part[1] + part[3]))
    rest.append(-CENTRE * part[3] - (HALF / 2) * part[2])
    rest.append(-(HALF / 2) * part[3])
    return part, rest


def combine_kernel(mom, v_hbm, s_hbm, outer, out, v, s, turn, sems):
    loads = []
    for c in range(3):
        loads.append((
            pltpu.make_async_copy(v_hbm.at[:, c], v.at[:, c], sems.at[0, c]),
            pltpu.make_async_copy(s_hbm.at[c], s.at[c], sems.at[1, c]),
        ))
    for pair in loads:
        for each in pair:
            each.start()
    line = jnp.sum(mom[...], axis=0, keepdims=True)
    lane = lax.broadcasted_iota(jnp.int32, (1, 128), 1)
    p = [jnp.sum(jnp.where(lane == k, line, 0.0), axis=1, keepdims=True) for k in range(8)]
    m = [p[0], p[1]] + [2.0 * p[k] - p[k % 2] for k in range(2, 8)]
    part, rest = coefficients(m)
    part = [jnp.broadcast_to(x, (8, 128)) for x in part]
    rest = [jnp.broadcast_to(x, (8, 128)) for x in rest]

    for c in range(3):
        for each in loads[c]:
            each.wait()

        def row(i, carry):
            for kx, k, tiles in PARTS:
                at = pl.ds(pl.multiple_of((kx * 8 + i) * 8, 8), 8)
                for b in range(WIDE):
                    vecs = [v[j, c, i, tiles.start + b] for j in range(5)]
                    slope = s[c, i, tiles.start + b]
                    weight = slope * slope + (stencil_diag * smoothing + damping)
                    turn[c, 0, FINE * b + k, at, :] = sum(part[j] * vecs[j] for j in range(4))
                    turn[c, 1, FINE * b + k, at, :] = weight * sum(rest[j] * vecs[j] for j in range(5))
            return carry

        lax.fori_loop(0, 8, row, 0)
        for e, i in ((0, 0), (1, 7)):
            for kx, k, tiles in PARTS:
                at = slice((kx * 8 + i) * 8, (kx * 8 + i) * 8 + 8)
                for b in range(WIDE):
                    m = tiles.start + b
                    slope = s[c, i, m]
                    weight = slope * slope + (stencil_diag * smoothing + damping)
                    turn[c, 1, FINE * b + k, at, :] += weight * rest[4] * outer[e, c, m * 8 : m * 8 + 8, :]
        for q in range(2):
            for dest in range(8):
                for kz in range(8):
                    lanes = slice(kz * 128, kz * 128 + 128)
                    out[dest, q, c, :, lanes] = turn[c, q, kz, pl.ds(dest, 16, stride=8), :].astype(BF16)


def combine(moments, vectors, slopes, outer):
    vmem = pl.BlockSpec(memory_space=pltpu.VMEM)
    hbm = pl.BlockSpec(memory_space=pltpu.HBM)
    return pl.pallas_call(
        combine_kernel,
        out_shape=jax.ShapeDtypeStruct((8, 2, 3, 16, 1024), BF16),
        in_specs=[vmem, hbm, hbm, vmem],
        out_specs=vmem,
        scratch_shapes=[
            pltpu.VMEM(vectors.shape, F32),
            pltpu.VMEM(slopes.shape, F32),
            pltpu.VMEM((3, 2, 8, 128, 128), F32),
            pltpu.SemaphoreType.DMA((2, 3)),
        ],
        compiler_params=pltpu.CompilerParams(vmem_limit_bytes=24 * 1024 * 1024),
        name="combine",
    )(moments, vectors, slopes, outer)


def finish_kernel(flip, back, perm, sol, res):
    lines = jnp.concatenate([back[src, q, 0] for q in range(2) for src in range(8)], axis=0)
    lines = jnp.concatenate([lines[:, b * SPAN : b * SPAN + SPAN] for b in range(WIDE)], axis=0)
    cells = lax.dot_general(lines, perm[...], (((1,), (1,)), ((), ())), preferred_element_type=F32)
    for b in range(WIDE):
        for q, out in ((0, sol), (1, res)):
            for src in range(8):
                rows = pl.ds(pl.multiple_of((src + flip[0] * (7 - 2 * src)) * 8, 8), 8)
                for kx in range(2):
                    at = b * 256 + q * 128 + src * 16 + kx * 8
                    out[0, kx, rows, b * SPAN : b * SPAN + SPAN] = cells[at : at + 8]


def finish(back, flip, perm):
    shape = jax.ShapeDtypeStruct((3, 2, 64, 1024), F32)
    spec = pl.BlockSpec((1, 2, 64, 1024), lambda c: (c, 0, 0, 0))
    return pl.pallas_call(
        finish_kernel,
        grid=(3,),
        out_shape=(shape, shape),
        in_specs=[
            pl.BlockSpec(memory_space=pltpu.SMEM),
            pl.BlockSpec((8, 2, 1, 16, 1024), lambda c: (0, 0, c, 0, 0)),
            pl.BlockSpec((SPAN, SPAN), lambda c: (0, 0)),
        ],
        out_specs=(spec, spec),
        compiler_params=pltpu.CompilerParams(vmem_limit_bytes=14 * 1024 * 1024),
        name="finish",
    )(flip, back, perm)


def exchange(cells, distance, inner):
    slabs, rows = lax.axis_size("slab"), lax.axis_size("row")

    def device(chunk):
        row, place = chunk // slabs, chunk % slabs
        return (place if row % 2 == 0 else slabs - 1 - place) * rows + row

    pairs = []
    for i in range(slabs * rows):
        low = (i // distance) % 2 == 0
        other = i + distance if low == inner else i - distance
        if 0 <= other < slabs * rows:
            pairs.append((device(i), device(other)))
    return lax.ppermute(cells, BOTH, pairs)


def per_device(moving, fixed, requests, footpoints, offset_x, offset_y, offset_z, fractions):
    depth, height, width = moving.shape
    perm = spread()
    block, slab = lax.axis_index("row"), lax.axis_index("slab")
    flip = block % 2
    start = block * height + (slab + flip * (7 - 2 * slab)) * 8 - 8
    peers, slots = requests.shape[2:]
    asked = jnp.pad(requests[0, 0], ((0, 0), (0, 128 - slots)))
    asked = lax.all_to_all(asked, BOTH, split_axis=0, concat_axis=0, tiled=True)
    outgoing = pick(asked, moving, slots)
    arrived = lax.all_to_all(outgoing, BOTH, split_axis=0, concat_axis=0, tiled=True)
    arrived = arrived.reshape(peers * slots, depth * TY, TZ)
    flip = flip.reshape(1)
    own = warp(
        arrived, footpoints[0, 0], offset_x[0, 0], offset_y[0, 0], offset_z[0, 0], fractions[0, 0], flip, fixed, perm
    )
    own = lax.all_to_all(own, "slab", split_axis=0, concat_axis=0, tiled=True)
    chunks = jnp.stack([exchange(own, 1, True), own, exchange(own, 1, False)])
    place = (slab + flip[0] * (7 - 2 * slab)).reshape(1)
    rows = start + jnp.arange(24, dtype=jnp.int32)
    rowmask = ((rows >= 0) & (rows < height * lax.axis_size("row"))).astype(F32)
    moments, vectors, slopes, ends = krylov(chunks, place, rowmask, peers)
    upper = place[0] // 2 % 2 == 1
    inwards = jnp.where(upper, own[:, 0:2, 0], own[:, 0:2, 7])
    outwards = jnp.where(upper, own[:, 0:2, 7], own[:, 0:2, 0])
    far = (exchange(inwards, 2, True), exchange(outwards, 2, False))
    moments, far = lax.optimization_barrier((moments, far))
    outer = outer_rows(ends, place, *far)
    moments, outer = lax.optimization_barrier((moments, outer))
    moments = lax.all_to_all(moments, BOTH, split_axis=0, concat_axis=0, tiled=True)
    back = combine(moments, vectors, slopes, outer)
    back = lax.all_to_all(back, "slab", split_axis=0, concat_axis=0, tiled=True)
    return finish(back, flip, perm)


def solution(mesh):
    return jax.shard_map(
        per_device,
        mesh=mesh,
        in_specs=(
            P("slab", "row", None),
            P("slab", "row", None),
            P("slab", "row", None, None),
            P("slab", "row", None, None),
            P("slab", "row", None),
            P("slab", "row", None),
            P("slab", "row", None),
            P("slab", "row", None, None),
        ),
        out_specs=(P(None, "slab", "row", None), P(None, "slab", "row", None)),
        check_vma=False,
    )
```

```python
import functools

import jax
import jax.numpy as jnp
from jax import lax
from jax.experimental import pallas as pl
from jax.experimental.pallas import tpu as pltpu
from jax.sharding import PartitionSpec as P

TY = 16
TZ = 128
ITERS = 4

smoothing = 0.02
damping = 0.1
stencil_diag = 42.0

LOW = 0.1
HIGH = 3.2
CENTRE = (HIGH + LOW) / 2
HALF = (HIGH - LOW) / 2
REACH = (smoothing / HALF) ** 4 * 8

FINE = 4
WIDE = 8 // FINE
SPAN = 128 * FINE

BOTH = ("slab", "row")
F32 = jnp.float32
BF16 = jnp.bfloat16


def spread():
    source = lax.broadcasted_iota(jnp.int32, (SPAN, SPAN), 0)
    target = lax.broadcasted_iota(jnp.int32, (SPAN, SPAN), 1)
    return (target == (source % FINE) * 128 + source // FINE).astype(BF16)


def pick_kernel(asked_hbm, moving, out, asked, block, buf, loads, stores):
    peers, slots, depth = buf.shape[:3]
    count = stores.shape[0]
    first = pltpu.make_async_copy(asked_hbm, asked, loads.at[0])
    second = pltpu.make_async_copy(moving, block, loads.at[1])
    first.start()
    second.start()
    first.wait()
    second.wait()

    def peer(p, carry):
        for slot in range(slots):
            number = asked[p, slot]
            tile = jnp.maximum(number, 0)
            rows = pl.ds(pl.multiple_of(lax.shift_right_logical(tile, 3) * TY, TY), TY)
            lanes = pl.ds(pl.multiple_of(lax.bitwise_and(tile, 7) * TZ, TZ), TZ)
            for x in range(depth):
                cells = block[x, rows, lanes]
                buf[p, slot, x] = jnp.where(number >= 0, cells, jnp.zeros_like(cells))
        return carry

    part = peers // count
    sent = []
    for i in range(count):
        lax.fori_loop(i * part, (i + 1) * part, peer, 0, unroll=8)
        mine = pl.ds(i * part, part)
        sent.append(pltpu.make_async_copy(buf.at[mine], out.at[mine], stores.at[i]))
        sent[-1].start()
    for each in sent:
        each.wait()


def pick(asked, moving, slots):
    hbm = pl.BlockSpec(memory_space=pltpu.HBM)
    shape = (asked.shape[0], slots, moving.shape[0], TY, TZ)
    return pl.pallas_call(
        pick_kernel,
        out_shape=jax.ShapeDtypeStruct(shape, BF16),
        in_specs=[hbm, hbm],
        out_specs=hbm,
        scratch_shapes=[
            pltpu.SMEM(asked.shape, jnp.int32),
            pltpu.VMEM(moving.shape, BF16),
            pltpu.VMEM(shape, BF16),
            pltpu.SemaphoreType.DMA((2,)),
            pltpu.SemaphoreType.DMA((4,)),
        ],
        compiler_params=pltpu.CompilerParams(vmem_limit_bytes=62 * 1024 * 1024),
        name="pick",
    )(asked, moving)


def warp_kernel(foot, ox, oy, oz, wts, flip, arrived, fixed, perm, out, nat):
    base_z = lax.broadcasted_iota(jnp.int32, (256, 128), 0) - lax.broadcasted_iota(jnp.int32, (256, 128), 1)
    ro = lax.broadcasted_iota(jnp.int32, (64, 128), 0)
    ci = lax.broadcasted_iota(jnp.int32, (64, 128), 1)
    same = (ro // 32 == ci // 64) & ((ro // 16) % 2 == (ci // 16) % 2)
    base_y = jnp.where(same, ((ci // 32) % 2) * 16 + ci % 16 - ro % 16, -1000)

    def band(base, shift, here, after):
        return jnp.where(base == shift, here, jnp.where(base == shift + 1, after, 0.0)).astype(BF16)

    def tile_row(j, carry):
        rows = pl.ds(pl.multiple_of(j * 16, 16), 16)
        firsts = []
        for k in range(8):
            t = j * 8 + k
            sides = []
            for c in range(2):
                corners = [arrived[foot[t * 8 + 4 * a + 2 * b + c]] for a in range(2) for b in range(2)]
                sides.append(jnp.concatenate(corners, axis=0))
            wz = band(base_z, oz[t], wts[t * 6 + 4], wts[t * 6 + 5])
            firsts.append(jnp.dot(jnp.concatenate(sides, axis=1), wz, preferred_element_type=F32).astype(BF16))
        seconds = []
        for k in range(8):
            t = j * 8 + k
            wy = band(base_y, oy[t], wts[t * 6 + 2], wts[t * 6 + 3])
            seconds.append(jnp.dot(wy, firsts[k], preferred_element_type=F32).astype(BF16).astype(F32))
        for k in range(8):
            t = j * 8 + k
            shift = ox[t]
            lanes = slice(k * 128, (k + 1) * 128)
            for xo in range(2):
                total = None
                for p in range(xo, xo + 3):
                    weight = jnp.where(
                        p - xo == shift, wts[t * 6], jnp.where(p - xo == shift + 1, wts[t * 6 + 1], 0.0)
                    )
                    term = weight * seconds[k][p * 16 : (p + 1) * 16]
                    total = term if total is None else total + term
                nat[xo, rows, lanes] = total.astype(BF16)
                nat[2 + xo, rows, lanes] = (total - fixed[xo, rows, lanes]).astype(BF16)
        return carry

    lax.fori_loop(0, 4, tile_row, 0)
    for b in range(WIDE):
        lanes = slice(b * SPAN, b * SPAN + SPAN)
        mixed = jnp.dot(nat[:, :, lanes].reshape(256, SPAN), perm[...], preferred_element_type=F32)
        for place in range(8):
            dest = place + flip[0] * (7 - 2 * place)
            for m in range(4):
                out[dest, m, :, lanes] = mixed[m * 64 + place * 8 : m * 64 + place * 8 + 8].astype(BF16)


def warp(arrived, footpoints, offset_x, offset_y, offset_z, fractions, flip, fixed, perm):
    near = lax.reduce_precision(1.0 - fractions, 8, 7)
    far = lax.reduce_precision(fractions, 8, 7)
    wts = jnp.stack([near, far], axis=-1).reshape(-1)
    smem = pl.BlockSpec(memory_space=pltpu.SMEM)
    vmem = pl.BlockSpec(memory_space=pltpu.VMEM)
    return pl.pallas_call(
        warp_kernel,
        out_shape=jax.ShapeDtypeStruct((8, 4, 8, 1024), BF16),
        in_specs=[smem] * 6 + [vmem] * 3,
        out_specs=vmem,
        scratch_shapes=[pltpu.VMEM((4, 64, 1024), BF16)],
        compiler_params=pltpu.CompilerParams(vmem_limit_bytes=10 * 1024 * 1024),
        name="warp",
    )(footpoints.reshape(-1), offset_x, offset_y, offset_z, wts, flip, arrived, fixed, perm)


PARTS = [
    (kx, k, slice(kx * 8 + k * WIDE, kx * 8 + k * WIDE + WIDE)) for kx in range(2) for k in range(FINE)
]


def edge_masks():
    sub = lax.broadcasted_iota(jnp.int32, (1, 8, 128), 1)
    lane = lax.broadcasted_iota(jnp.int32, (WIDE, 8, 128), 2)
    one = lambda flag: jnp.where(flag, 1.0, 0.0).astype(F32)
    return one(sub != 0), one(sub != 7), lane == 0, lane == 127


def load(ref, *at):
    return {(kx, k): ref[(*at, tiles)] for kx, k, tiles in PARTS}


def x_pair(v, kx, k, masks):
    other = v[1 - kx, k]
    if kx == 0:
        return pltpu.roll(other, 1, 1) * masks[0], other
    return other, pltpu.roll(other, 7, 1) * masks[1]


def z_pair(v, kx, k, masks):
    nothing = jnp.zeros((1, 8, 128), F32)
    if k > 0:
        before = v[kx, k - 1]
    else:
        turned = pltpu.roll(v[kx, FINE - 1], 1, 2)
        carried = jnp.concatenate([nothing, turned[: WIDE - 1]], axis=0) if WIDE > 1 else nothing
        before = jnp.where(masks[2], carried, turned)
    if k < FINE - 1:
        after = v[kx, k + 1]
    else:
        turned = pltpu.roll(v[kx, 0], 127, 2)
        carried = jnp.concatenate([turned[1:], nothing], axis=0) if WIDE > 1 else nothing
        after = jnp.where(masks[3], carried, turned)
    return before, after


def beside(v, kx, k, masks):
    x0, x1 = x_pair(v, kx, k, masks)
    z0, z1 = z_pair(v, kx, k, masks)
    return (x0 + x1) + (z0 + z1)


def field(rows):
    return pltpu.VMEM((3, rows, 16, 8, 128), F32)


def krylov_kernel(place, rowmask, chunks, mom, vout, sout, ends, s_s, im_s, v0, v1, v2, sems):
    masks = edge_masks()

    def chain(c, tiles, end, step):
        one = im_s[c, end, tiles] * im_s[c, end - step, tiles]
        return one * (im_s[c, end - 2 * step, tiles] * im_s[c, end - 3 * step, tiles]) * REACH

    def prepare(d_s, w_s):
        odd = lax.bitwise_and(place[0], 1)
        sources = (2 - 2 * odd, 1, 2 * odd)
        for g in range(3):
            for src in range(8):
                lines = chunks[sources[g], src].astype(F32).reshape(32, 1024)
                for kz in range(8):
                    d_s[kz, src * 96 + g * 32 : src * 96 + g * 32 + 32, :] = lines[:, kz * 128 : kz * 128 + 128]

        def fetch(row, k, b):
            return d_s[FINE * b + k, pl.ds(row, 8, stride=96), :]

        def line(n, m):
            return lax.shift_right_logical(n, 3) * 32 + m * 8 + lax.bitwise_and(n, 7)

        def put_w(i, row_of):
            for kx, k, tiles in PARTS:
                for b in range(WIDE):
                    w_s[i, tiles.start + b] = fetch(row_of(kx), k, b)

        def fill(n, carry):
            put_w(n, lambda kx: line(n, kx))
            return carry

        lax.fori_loop(0, 24, fill, 0, unroll=4)

        def begin(n, carry):
            w = load(w_s, n)
            keep = rowmask[n]
            for kx, k, tiles in PARTS:
                diff = jnp.stack([fetch(line(n, 2 + kx), k, b) for b in range(WIDE)])
                xb, xa = x_pair(w, kx, k, masks)
                zb, za = z_pair(w, kx, k, masks)
                ys = w_s[n + 1, tiles] - w_s[n - 1, tiles]
                for c, s in enumerate(((xa - xb) * 0.5, ys * 0.5, (za - zb) * 0.5)):
                    im = keep / (s * s + (stencil_diag * smoothing + damping))
                    s_s[c, n, tiles] = s
                    im_s[c, n, tiles] = im
                    v0[c, n, tiles] = -s * diff * im
            return carry

        for c in range(3):
            for n in (0, 23):
                v0[c, n] = jnp.zeros((16, 8, 128), F32)
        lax.fori_loop(1, 23, begin, 0, unroll=2)

        for e, (edge, step) in enumerate(((0, 2), (23, -2))):
            w = load(w_s, edge)
            for kx, k, tiles in PARTS:
                lines = slice(tiles.start * 8, tiles.stop * 8)
                diff = jnp.stack([fetch(line(edge, 2 + kx), k, b) for b in range(WIDE)])
                xb, xa = x_pair(w, kx, k, masks)
                zb, za = z_pair(w, kx, k, masks)
                for slot, c, s in ((0, 0, (xa - xb) * 0.5), (1, 2, (za - zb) * 0.5)):
                    start = -s * diff / (s * s + (stencil_diag * smoothing + damping))
                    value = chain(c, tiles, edge + 4 * step, step) * start * rowmask[edge]
                    ends[e, slot, lines, :] = value.reshape(WIDE * 8, 128)
                ends[e, 2, lines, :] = (chain(1, tiles, edge + 4 * step, step) * rowmask[edge]).reshape(WIDE * 8, 128)
                ends[e, 3, lines, :] = w_s[edge + step // 2, tiles].reshape(WIDE * 8, 128)
                ends[e, 4, lines, :] = diff.reshape(WIDE * 8, 128)

    def iterate(u_s, v3, v4):
        vs = [v0, v1, v2, v3, v4]

        def copy(j):
            return pltpu.make_async_copy(vs[j].at[:, pl.ds(8 - 2 * j, 8)], vout.at[j], sems.at[j])

        s_copy = pltpu.make_async_copy(s_s.at[:, pl.ds(8, 8)], sout, sems.at[5])
        s_copy.start()
        copy(0).start()

        for j in range(4):
            gain = (1.0 if j == 0 else 2.0) / HALF
            old, new = vs[j], vs[j + 1]
            off = 2 * j

            def first(n, carry):
                scale = rowmask[n] * (gain * smoothing)
                for c in range(3):
                    v = load(old, c, n - off)
                    for kx, k, tiles in PARTS:
                        total = beside(v, kx, k, masks) + (old[c, n - off - 1, tiles] + old[c, n - off + 1, tiles])
                        u_s[c, n - 1, tiles] = (6.0 * v[kx, k] - total) * scale
                return carry

            lax.fori_loop(off + 1, 23 - off, first, 0, unroll=2)

            def second(n, carry):
                dots = {}
                for kx, k, tiles in PARTS:
                    dot = s_s[0, n, tiles] * old[0, n - off, tiles]
                    dot = dot + s_s[1, n, tiles] * old[1, n - off, tiles]
                    dots[kx, k] = (dot + s_s[2, n, tiles] * old[2, n - off, tiles]) * gain
                for c in range(3):
                    u = load(u_s, c, n - 1)
                    for kx, k, tiles in PARTS:
                        total = beside(u, kx, k, masks) + (u_s[c, n - 2, tiles] + u_s[c, n, tiles])
                        v = old[c, n - off, tiles]
                        image = s_s[c, n, tiles] * dots[kx, k] + (6.0 * u[kx, k] - total) + (gain * damping) * v
                        value = im_s[c, n, tiles] * image - (gain * CENTRE) * v
                        if j > 0:
                            value = value - vs[j - 1][c, n - off + 2, tiles]
                        new[c, n - off - 2, tiles] = value
                return carry

            lax.fori_loop(off + 2, 22 - off, second, 0, unroll=2)
            copy(j + 1).start()

        def products(n, sums):
            sums = list(sums)
            for c in range(3):
                for kx, k, tiles in PARTS:
                    s = s_s[c, n, tiles]
                    m = s * s + (stencil_diag * smoothing + damping)
                    v = [vs[j][c, n - 2 * j, tiles] for j in range(5)]
                    for j in range(4):
                        t = m * v[j]
                        for q, other in ((2 * j, v[j]), (2 * j + 1, v[j + 1])):
                            sums[q] = sums[q] + jnp.sum(t * other, axis=0)
            return tuple(sums)

        sums = list(lax.fori_loop(8, 16, products, tuple(jnp.zeros((8, 128), F32) for _ in range(8)), unroll=2))
        for first_row, step in ((8, 2), (15, -2)):
            end = first_row + 4 * step
            for c in range(3):
                for kx, k, tiles in PARTS:
                    share = chain(c, tiles, end, step) * v0[c, first_row, tiles]
                    s = s_s[c, end, tiles]
                    m = s * s + (stencil_diag * smoothing + damping)
                    sums[7] = sums[7] + jnp.sum(m * share * v3[c, end - 6, tiles], axis=0)
        lane = lax.broadcasted_iota(jnp.int32, (1, 128), 1)
        out = jnp.zeros((1, 128), F32)
        for q in range(8):
            out = jnp.where(lane == q, jnp.sum(sums[q], keepdims=True), out)
        mom[...] = jnp.broadcast_to(out, mom.shape)
        s_copy.wait()
        for j in range(5):
            copy(j).wait()

    pl.run_scoped(
        prepare,
        pltpu.VMEM((8, 768, 128), F32),
        pltpu.VMEM((24, 16, 8, 128), F32),
    )
    pl.run_scoped(iterate, field(22), field(12), field(8))


def krylov(chunks, place, rowmask, peers):
    vmem = pl.BlockSpec(memory_space=pltpu.VMEM)
    hbm = pl.BlockSpec(memory_space=pltpu.HBM)

    return pl.pallas_call(
        krylov_kernel,
        out_shape=(
            jax.ShapeDtypeStruct((peers, 128), F32),
            jax.ShapeDtypeStruct((5, 3, 8, 16, 8, 128), F32),
            jax.ShapeDtypeStruct((3, 8, 16, 8, 128), F32),
            jax.ShapeDtypeStruct((2, 5, 128, 128), F32),
        ),
        in_specs=[pl.BlockSpec(memory_space=pltpu.SMEM)] * 2 + [vmem],
        out_specs=(vmem, hbm, hbm, vmem),
        scratch_shapes=[
            field(24),
            field(24),
            field(24),
            field(20),
            field(16),
            pltpu.SemaphoreType.DMA((6,)),
        ],
        compiler_params=pltpu.CompilerParams(vmem_limit_bytes=33 * 1024 * 1024),
        cost_estimate=pl.CostEstimate(flops=400_000_000, bytes_accessed=60_000_000, transcendentals=0),
        name="krylov",
    )(place, rowmask, chunks)


def ends_kernel(place, ends, inner, outer, out, rows):
    upper = lax.bitwise_and(place[0], 2) == 2
    both = [x[...].astype(F32).reshape(16, 1024) for x in (inner, outer)]
    for e in range(2):
        lines = jnp.where(upper, both[e], both[1 - e])
        for kz in range(8):
            rows[kz] = lines[:, kz * 128 : kz * 128 + 128]
        for slot, c in ((0, 0), (1, 2)):
            out[e, c] = ends[e, slot]
        for kx, k, tiles in PARTS:
            for b in range(WIDE):
                at = slice((tiles.start + b) * 8, (tiles.start + b) * 8 + 8)
                beyond = rows[FINE * b + k, pl.ds(kx, 8, stride=2), :]
                near = ends[e, 3, at, :]
                s = (near - beyond) * 0.5 if e == 0 else (beyond - near) * 0.5
                start = -s * ends[e, 4, at, :] / (s * s + (stencil_diag * smoothing + damping))
                out[e, 1, at, :] = ends[e, 2, at, :] * start


def outer_rows(ends, place, inner, outer):
    vmem = pl.BlockSpec(memory_space=pltpu.VMEM)
    return pl.pallas_call(
        ends_kernel,
        out_shape=jax.ShapeDtypeStruct((2, 3, 128, 128), F32),
        in_specs=[pl.BlockSpec(memory_space=pltpu.SMEM)] + [vmem] * 3,
        out_specs=vmem,
        scratch_shapes=[pltpu.VMEM((8, 16, 128), F32)],
        compiler_params=pltpu.CompilerParams(vmem_limit_bytes=4 * 1024 * 1024),
        name="outer_rows",
    )(place, ends, inner, outer)


def coefficients(m):
    def lam(k):
        if k == 0:
            return CENTRE * m[0] + HALF * m[1]
        return CENTRE * m[k] + (HALF / 2) * (m[k + 1] + m[k - 1])

    lams = [lam(k) for k in range(7)]
    rows = [[0.5 * (lams[i + j] + lams[abs(i - j)]) for j in range(4)] + [m[i]] for i in range(4)]
    for p in range(4):
        inverse = 1.0 / rows[p][p]
        for q in range(p + 1, 4):
            factor = rows[q][p] * inverse
            rows[q] = [rows[q][k] - factor * rows[p][k] if k > p else rows[q][k] for k in range(5)]
    part = [None] * 4
    for p in reversed(range(4)):
        value = rows[p][4]
        for q in range(p + 1, 4):
            value = value - rows[p][q] * part[q]
        part[p] = value / rows[p][p]
    rest = [1.0 - CENTRE * part[0] - (HALF / 2) * part[1]]
    rest.append(-CENTRE * part[1] - HALF * part[0] - (HALF / 2) * part[2])
    rest.append(-CENTRE * part[2] - (HALF / 2) * (part[1] + part[3]))
    rest.append(-CENTRE * part[3] - (HALF / 2) * part[2])
    rest.append(-(HALF / 2) * part[3])
    return part, rest


def combine_kernel(mom, v, s, outer, out, turn):
    line = jnp.sum(mom[...], axis=0, keepdims=True)
    lane = lax.broadcasted_iota(jnp.int32, (1, 128), 1)
    p = [jnp.sum(jnp.where(lane == k, line, 0.0), axis=1, keepdims=True) for k in range(8)]
    m = [p[0], p[1]] + [2.0 * p[k] - p[k % 2] for k in range(2, 8)]
    part, rest = coefficients(m)
    part = [jnp.broadcast_to(x, (8, 128)) for x in part]
    rest = [jnp.broadcast_to(x, (8, 128)) for x in rest]

    for c in range(3):

        def row(i, carry):
            for kx, k, tiles in PARTS:
                at = pl.ds(pl.multiple_of((kx * 8 + i) * 8, 8), 8)
                for b in range(WIDE):
                    vecs = [v[j, c, i, tiles.start + b] for j in range(5)]
                    slope = s[c, i, tiles.start + b]
                    weight = slope * slope + (stencil_diag * smoothing + damping)
                    turn[c, 0, FINE * b + k, at, :] = sum(part[j] * vecs[j] for j in range(4))
                    turn[c, 1, FINE * b + k, at, :] = weight * sum(rest[j] * vecs[j] for j in range(5))
            return carry

        lax.fori_loop(0, 8, row, 0)
        for e, i in ((0, 0), (1, 7)):
            for kx, k, tiles in PARTS:
                at = slice((kx * 8 + i) * 8, (kx * 8 + i) * 8 + 8)
                for b in range(WIDE):
                    m = tiles.start + b
                    slope = s[c, i, m]
                    weight = slope * slope + (stencil_diag * smoothing + damping)
                    turn[c, 1, FINE * b + k, at, :] += weight * rest[4] * outer[e, c, m * 8 : m * 8 + 8, :]
        for q in range(2):
            for dest in range(8):
                for kz in range(8):
                    lanes = slice(kz * 128, kz * 128 + 128)
                    out[dest, q, c, :, lanes] = turn[c, q, kz, pl.ds(dest, 16, stride=8), :].astype(BF16)


def combine(moments, vectors, slopes, outer):
    vmem = pl.BlockSpec(memory_space=pltpu.VMEM)
    return pl.pallas_call(
        combine_kernel,
        out_shape=jax.ShapeDtypeStruct((8, 2, 3, 16, 1024), BF16),
        in_specs=[vmem] * 4,
        out_specs=vmem,
        scratch_shapes=[pltpu.VMEM((3, 2, 8, 128, 128), F32)],
        compiler_params=pltpu.CompilerParams(vmem_limit_bytes=24 * 1024 * 1024),
        name="combine",
    )(moments, vectors, slopes, outer)


def finish_kernel(flip, back, perm, sol, res, cells_s, sems):
    stores = []
    for c in range(3):
        lines = jnp.concatenate([back[src, q, c] for q in range(2) for src in range(8)], axis=0)
        lines = jnp.concatenate([lines[:, b * SPAN : b * SPAN + SPAN] for b in range(WIDE)], axis=0)
        cells = lax.dot_general(lines, perm[...], (((1,), (1,)), ((), ())), preferred_element_type=F32)
        for q, out in ((0, sol), (1, res)):
            for b in range(WIDE):
                for src in range(8):
                    rows = pl.ds(pl.multiple_of((src + flip[0] * (7 - 2 * src)) * 8, 8), 8)
                    for kx in range(2):
                        at = b * 256 + q * 128 + src * 16 + kx * 8
                        cells_s[q, c, kx, rows, b * SPAN : b * SPAN + SPAN] = cells[at : at + 8]
            stores.append(pltpu.make_async_copy(cells_s.at[q, c], out.at[c], sems.at[q, c]))
            stores[-1].start()
    for each in stores:
        each.wait()


def finish(back, flip, perm):
    shape = jax.ShapeDtypeStruct((3, 2, 64, 1024), F32)
    vmem = pl.BlockSpec(memory_space=pltpu.VMEM)
    hbm = pl.BlockSpec(memory_space=pltpu.HBM)
    return pl.pallas_call(
        finish_kernel,
        out_shape=(shape, shape),
        in_specs=[pl.BlockSpec(memory_space=pltpu.SMEM), vmem, vmem],
        out_specs=(hbm, hbm),
        scratch_shapes=[pltpu.VMEM((2, *shape.shape), F32), pltpu.SemaphoreType.DMA((2, 3))],
        compiler_params=pltpu.CompilerParams(vmem_limit_bytes=24 * 1024 * 1024),
        name="finish",
    )(flip, back, perm)


def exchange(cells, distance, inner):
    slabs, rows = lax.axis_size("slab"), lax.axis_size("row")

    def device(chunk):
        row, place = chunk // slabs, chunk % slabs
        return (place if row % 2 == 0 else slabs - 1 - place) * rows + row

    pairs = []
    for i in range(slabs * rows):
        low = (i // distance) % 2 == 0
        other = i + distance if low == inner else i - distance
        if 0 <= other < slabs * rows:
            pairs.append((device(i), device(other)))
    return lax.ppermute(cells, BOTH, pairs)


def per_device(moving, fixed, requests, footpoints, offset_x, offset_y, offset_z, fractions):
    depth, height, width = moving.shape
    perm = spread()
    block, slab = lax.axis_index("row"), lax.axis_index("slab")
    flip = block % 2
    start = block * height + (slab + flip * (7 - 2 * slab)) * 8 - 8
    peers, slots = requests.shape[2:]
    asked = jnp.pad(requests[0, 0], ((0, 0), (0, 128 - slots)))
    asked = lax.all_to_all(asked, BOTH, split_axis=0, concat_axis=0, tiled=True)
    outgoing = pick(asked, moving, slots)
    arrived = lax.all_to_all(outgoing, BOTH, split_axis=0, concat_axis=0, tiled=True)
    arrived = arrived.reshape(peers * slots, depth * TY, TZ)
    flip = flip.reshape(1)
    own = warp(
        arrived, footpoints[0, 0], offset_x[0, 0], offset_y[0, 0], offset_z[0, 0], fractions[0, 0], flip, fixed, perm
    )
    own = lax.all_to_all(own, "slab", split_axis=0, concat_axis=0, tiled=True)
    chunks = jnp.stack([exchange(own, 1, True), own, exchange(own, 1, False)])
    place = (slab + flip[0] * (7 - 2 * slab)).reshape(1)
    rows = start + jnp.arange(24, dtype=jnp.int32)
    rowmask = ((rows >= 0) & (rows < height * lax.axis_size("row"))).astype(F32)
    moments, vectors, slopes, ends = krylov(chunks, place, rowmask, peers)
    upper = place[0] // 2 % 2 == 1
    inwards = jnp.where(upper, own[:, 0:2, 0], own[:, 0:2, 7])
    outwards = jnp.where(upper, own[:, 0:2, 7], own[:, 0:2, 0])
    far = (exchange(inwards, 2, True), exchange(outwards, 2, False))
    moments, far = lax.optimization_barrier((moments, far))
    outer = outer_rows(ends, place, *far)
    moments, outer = lax.optimization_barrier((moments, outer))
    moments = lax.all_to_all(moments, BOTH, split_axis=0, concat_axis=0, tiled=True)
    back = combine(moments, vectors, slopes, outer)
    back = lax.all_to_all(back, "slab", split_axis=0, concat_axis=0, tiled=True)
    return finish(back, flip, perm)


def solution(mesh):
    return jax.shard_map(
        per_device,
        mesh=mesh,
        in_specs=(
            P("slab", "row", None),
            P("slab", "row", None),
            P("slab", "row", None, None),
            P("slab", "row", None, None),
            P("slab", "row", None),
            P("slab", "row", None),
            P("slab", "row", None),
            P("slab", "row", None, None),
        ),
        out_specs=(P(None, "slab", "row", None), P(None, "slab", "row", None)),
        check_vma=False,
    )
```

```python
import functools

import jax
import jax.numpy as jnp
from jax import lax
from jax.experimental import pallas as pl
from jax.experimental.pallas import tpu as pltpu
from jax.sharding import PartitionSpec as P

TY = 16
TZ = 128
ITERS = 4

smoothing = 0.02
damping = 0.1
stencil_diag = 42.0

LOW = 0.1
HIGH = 3.2
CENTRE = (HIGH + LOW) / 2
HALF = (HIGH - LOW) / 2
REACH = (smoothing / HALF) ** 4 * 8

FINE = 4
WIDE = 8 // FINE
SPAN = 128 * FINE

BOTH = ("slab", "row")
F32 = jnp.float32
BF16 = jnp.bfloat16


def spread():
    source = lax.broadcasted_iota(jnp.int32, (SPAN, SPAN), 0)
    target = lax.broadcasted_iota(jnp.int32, (SPAN, SPAN), 1)
    return (target == (source % FINE) * 128 + source // FINE).astype(BF16)


def pick_kernel(asked_hbm, moving, out, asked, block, buf, loads, stores):
    peers, slots, depth = buf.shape[:3]
    count = stores.shape[0]
    first = pltpu.make_async_copy(asked_hbm, asked, loads.at[0])
    second = pltpu.make_async_copy(moving, block, loads.at[1])
    first.start()
    second.start()
    first.wait()
    second.wait()

    def peer(p, carry):
        for slot in range(slots):
            number = asked[p, slot]
            tile = jnp.maximum(number, 0)
            rows = pl.ds(pl.multiple_of(lax.shift_right_logical(tile, 3) * TY, TY), TY)
            lanes = pl.ds(pl.multiple_of(lax.bitwise_and(tile, 7) * TZ, TZ), TZ)
            for x in range(depth):
                cells = block[x, rows, lanes]
                buf[p, slot, x] = jnp.where(number >= 0, cells, jnp.zeros_like(cells))
        return carry

    part = peers // count
    sent = []
    for i in range(count):
        lax.fori_loop(i * part, (i + 1) * part, peer, 0, unroll=8)
        mine = pl.ds(i * part, part)
        sent.append(pltpu.make_async_copy(buf.at[mine], out.at[mine], stores.at[i]))
        sent[-1].start()
    for each in sent:
        each.wait()


def pick(asked, moving, slots):
    hbm = pl.BlockSpec(memory_space=pltpu.HBM)
    shape = (asked.shape[0], slots, moving.shape[0], TY, TZ)
    return pl.pallas_call(
        pick_kernel,
        out_shape=jax.ShapeDtypeStruct(shape, BF16),
        in_specs=[hbm, hbm],
        out_specs=hbm,
        scratch_shapes=[
            pltpu.SMEM(asked.shape, jnp.int32),
            pltpu.VMEM(moving.shape, BF16),
            pltpu.VMEM(shape, BF16),
            pltpu.SemaphoreType.DMA((2,)),
            pltpu.SemaphoreType.DMA((4,)),
        ],
        compiler_params=pltpu.CompilerParams(vmem_limit_bytes=62 * 1024 * 1024),
        name="pick",
    )(asked, moving)


def warp_kernel(foot, ox, oy, oz, wts, flip, arrived, fixed, perm, out, nat):
    base_z = lax.broadcasted_iota(jnp.int32, (256, 128), 0) - lax.broadcasted_iota(jnp.int32, (256, 128), 1)
    ro = lax.broadcasted_iota(jnp.int32, (64, 128), 0)
    ci = lax.broadcasted_iota(jnp.int32, (64, 128), 1)
    same = (ro // 32 == ci // 64) & ((ro // 16) % 2 == (ci // 16) % 2)
    base_y = jnp.where(same, ((ci // 32) % 2) * 16 + ci % 16 - ro % 16, -1000)

    def band(base, shift, here, after):
        return jnp.where(base == shift, here, jnp.where(base == shift + 1, after, 0.0)).astype(BF16)

    def tile_row(j, carry):
        rows = pl.ds(pl.multiple_of(j * 16, 16), 16)
        firsts = []
        for k in range(8):
            t = j * 8 + k
            sides = []
            for c in range(2):
                corners = [arrived[foot[t * 8 + 4 * a + 2 * b + c]] for a in range(2) for b in range(2)]
                sides.append(jnp.concatenate(corners, axis=0))
            wz = band(base_z, oz[t], wts[t * 6 + 4], wts[t * 6 + 5])
            firsts.append(jnp.dot(jnp.concatenate(sides, axis=1), wz, preferred_element_type=F32).astype(BF16))
        seconds = []
        for k in range(8):
            t = j * 8 + k
            wy = band(base_y, oy[t], wts[t * 6 + 2], wts[t * 6 + 3])
            seconds.append(jnp.dot(wy, firsts[k], preferred_element_type=F32).astype(BF16).astype(F32))
        for k in range(8):
            t = j * 8 + k
            shift = ox[t]
            lanes = slice(k * 128, (k + 1) * 128)
            for xo in range(2):
                total = None
                for p in range(xo, xo + 3):
                    weight = jnp.where(
                        p - xo == shift, wts[t * 6], jnp.where(p - xo == shift + 1, wts[t * 6 + 1], 0.0)
                    )
                    term = weight * seconds[k][p * 16 : (p + 1) * 16]
                    total = term if total is None else total + term
                nat[xo, rows, lanes] = total.astype(BF16)
                nat[2 + xo, rows, lanes] = (total - fixed[xo, rows, lanes]).astype(BF16)
        return carry

    lax.fori_loop(0, 4, tile_row, 0)
    for b in range(WIDE):
        lanes = slice(b * SPAN, b * SPAN + SPAN)
        mixed = jnp.dot(nat[:, :, lanes].reshape(256, SPAN), perm[...], preferred_element_type=F32)
        for place in range(8):
            dest = place + flip[0] * (7 - 2 * place)
            for m in range(4):
                out[dest, m, :, lanes] = mixed[m * 64 + place * 8 : m * 64 + place * 8 + 8].astype(BF16)


def warp(arrived, footpoints, offset_x, offset_y, offset_z, fractions, flip, fixed, perm):
    near = lax.reduce_precision(1.0 - fractions, 8, 7)
    far = lax.reduce_precision(fractions, 8, 7)
    wts = jnp.stack([near, far], axis=-1).reshape(-1)
    smem = pl.BlockSpec(memory_space=pltpu.SMEM)
    vmem = pl.BlockSpec(memory_space=pltpu.VMEM)
    return pl.pallas_call(
        warp_kernel,
        out_shape=jax.ShapeDtypeStruct((8, 4, 8, 1024), BF16),
        in_specs=[smem] * 6 + [vmem] * 3,
        out_specs=vmem,
        scratch_shapes=[pltpu.VMEM((4, 64, 1024), BF16)],
        compiler_params=pltpu.CompilerParams(vmem_limit_bytes=10 * 1024 * 1024),
        name="warp",
    )(footpoints.reshape(-1), offset_x, offset_y, offset_z, wts, flip, arrived, fixed, perm)


PARTS = [
    (kx, k, slice(kx * 8 + k * WIDE, kx * 8 + k * WIDE + WIDE)) for kx in range(2) for k in range(FINE)
]


def edge_masks():
    sub = lax.broadcasted_iota(jnp.int32, (1, 8, 128), 1)
    lane = lax.broadcasted_iota(jnp.int32, (WIDE, 8, 128), 2)
    one = lambda flag: jnp.where(flag, 1.0, 0.0).astype(F32)
    return one(sub != 0), one(sub != 7), lane == 0, lane == 127


def load(ref, *at):
    return {(kx, k): ref[(*at, tiles)] for kx, k, tiles in PARTS}


def x_pair(v, kx, k, masks):
    other = v[1 - kx, k]
    if kx == 0:
        return pltpu.roll(other, 1, 1) * masks[0], other
    return other, pltpu.roll(other, 7, 1) * masks[1]


def z_pair(v, kx, k, masks):
    nothing = jnp.zeros((1, 8, 128), F32)
    if k > 0:
        before = v[kx, k - 1]
    else:
        turned = pltpu.roll(v[kx, FINE - 1], 1, 2)
        carried = jnp.concatenate([nothing, turned[: WIDE - 1]], axis=0) if WIDE > 1 else nothing
        before = jnp.where(masks[2], carried, turned)
    if k < FINE - 1:
        after = v[kx, k + 1]
    else:
        turned = pltpu.roll(v[kx, 0], 127, 2)
        carried = jnp.concatenate([turned[1:], nothing], axis=0) if WIDE > 1 else nothing
        after = jnp.where(masks[3], carried, turned)
    return before, after


def beside(v, kx, k, masks):
    x0, x1 = x_pair(v, kx, k, masks)
    z0, z1 = z_pair(v, kx, k, masks)
    return (x0 + x1) + (z0 + z1)


def field(rows):
    return pltpu.VMEM((3, rows, 16, 8, 128), F32)


def krylov_kernel(place, rowmask, chunks, mom, vout, sout, ends, v4, s_s, im_s, v0, v1, v2, sems):
    masks = edge_masks()

    def chain(c, tiles, end, step):
        one = im_s[c, end, tiles] * im_s[c, end - step, tiles]
        return one * (im_s[c, end - 2 * step, tiles] * im_s[c, end - 3 * step, tiles]) * REACH

    def prepare(d_s, w_s):
        odd = lax.bitwise_and(place[0], 1)
        sources = (2 - 2 * odd, 1, 2 * odd)
        for g in range(3):
            for src in range(8):
                lines = chunks[sources[g], src].astype(F32).reshape(32, 1024)
                for kz in range(8):
                    d_s[kz, src * 96 + g * 32 : src * 96 + g * 32 + 32, :] = lines[:, kz * 128 : kz * 128 + 128]

        def fetch(row, k, b):
            return d_s[FINE * b + k, pl.ds(row, 8, stride=96), :]

        def line(n, m):
            return lax.shift_right_logical(n, 3) * 32 + m * 8 + lax.bitwise_and(n, 7)

        def put_w(i, row_of):
            for kx, k, tiles in PARTS:
                for b in range(WIDE):
                    w_s[i, tiles.start + b] = fetch(row_of(kx), k, b)

        def fill(n, carry):
            put_w(n, lambda kx: line(n, kx))
            return carry

        lax.fori_loop(0, 24, fill, 0, unroll=4)

        def begin(n, carry):
            w = load(w_s, n)
            keep = rowmask[n]
            for kx, k, tiles in PARTS:
                diff = jnp.stack([fetch(line(n, 2 + kx), k, b) for b in range(WIDE)])
                xb, xa = x_pair(w, kx, k, masks)
                zb, za = z_pair(w, kx, k, masks)
                ys = w_s[n + 1, tiles] - w_s[n - 1, tiles]
                for c, s in enumerate(((xa - xb) * 0.5, ys * 0.5, (za - zb) * 0.5)):
                    im = keep / (s * s + (stencil_diag * smoothing + damping))
                    s_s[c, n, tiles] = s
                    im_s[c, n, tiles] = im
                    v0[c, n, tiles] = -s * diff * im
            return carry

        for c in range(3):
            for n in (0, 23):
                v0[c, n] = jnp.zeros((16, 8, 128), F32)
        lax.fori_loop(1, 23, begin, 0, unroll=2)

        for e, (edge, step) in enumerate(((0, 2), (23, -2))):
            w = load(w_s, edge)
            for kx, k, tiles in PARTS:
                lines = slice(tiles.start * 8, tiles.stop * 8)
                diff = jnp.stack([fetch(line(edge, 2 + kx), k, b) for b in range(WIDE)])
                xb, xa = x_pair(w, kx, k, masks)
                zb, za = z_pair(w, kx, k, masks)
                for slot, c, s in ((0, 0, (xa - xb) * 0.5), (1, 2, (za - zb) * 0.5)):
                    start = -s * diff / (s * s + (stencil_diag * smoothing + damping))
                    value = chain(c, tiles, edge + 4 * step, step) * start * rowmask[edge]
                    ends[e, slot, lines, :] = value.reshape(WIDE * 8, 128)
                ends[e, 2, lines, :] = (chain(1, tiles, edge + 4 * step, step) * rowmask[edge]).reshape(WIDE * 8, 128)
                ends[e, 3, lines, :] = w_s[edge + step // 2, tiles].reshape(WIDE * 8, 128)
                ends[e, 4, lines, :] = diff.reshape(WIDE * 8, 128)

    def iterate(u_s, v3):
        vs = [v0, v1, v2, v3, v4]

        def copy(j):
            return pltpu.make_async_copy(vs[j].at[:, pl.ds(8 - 2 * j, 8)], vout.at[j], sems.at[j])

        s_copy = pltpu.make_async_copy(s_s.at[:, pl.ds(8, 8)], sout, sems.at[5])
        s_copy.start()
        copy(0).start()

        for j in range(4):
            gain = (1.0 if j == 0 else 2.0) / HALF
            old, new = vs[j], vs[j + 1]
            off = 2 * j

            def first(n, carry):
                scale = rowmask[n] * (gain * smoothing)
                for c in range(3):
                    v = load(old, c, n - off)
                    for kx, k, tiles in PARTS:
                        total = beside(v, kx, k, masks) + (old[c, n - off - 1, tiles] + old[c, n - off + 1, tiles])
                        u_s[c, n - 1, tiles] = (6.0 * v[kx, k] - total) * scale
                return carry

            lax.fori_loop(off + 1, 23 - off, first, 0, unroll=2)

            def second(n, carry):
                dots = {}
                for kx, k, tiles in PARTS:
                    dot = s_s[0, n, tiles] * old[0, n - off, tiles]
                    dot = dot + s_s[1, n, tiles] * old[1, n - off, tiles]
                    dots[kx, k] = (dot + s_s[2, n, tiles] * old[2, n - off, tiles]) * gain
                for c in range(3):
                    u = load(u_s, c, n - 1)
                    for kx, k, tiles in PARTS:
                        total = beside(u, kx, k, masks) + (u_s[c, n - 2, tiles] + u_s[c, n, tiles])
                        v = old[c, n - off, tiles]
                        image = s_s[c, n, tiles] * dots[kx, k] + (6.0 * u[kx, k] - total) + (gain * damping) * v
                        value = im_s[c, n, tiles] * image - (gain * CENTRE) * v
                        if j > 0:
                            value = value - vs[j - 1][c, n - off + 2, tiles]
                        new[c, n - off - 2, tiles] = value
                return carry

            lax.fori_loop(off + 2, 22 - off, second, 0, unroll=2)
            if j < 3:
                copy(j + 1).start()

        def products(n, sums):
            sums = list(sums)
            for c in range(3):
                for kx, k, tiles in PARTS:
                    s = s_s[c, n, tiles]
                    m = s * s + (stencil_diag * smoothing + damping)
                    v = [vs[j][c, n - 2 * j, tiles] for j in range(5)]
                    for j in range(4):
                        t = m * v[j]
                        for q, other in ((2 * j, v[j]), (2 * j + 1, v[j + 1])):
                            sums[q] = sums[q] + jnp.sum(t * other, axis=0)
            return tuple(sums)

        sums = list(lax.fori_loop(8, 16, products, tuple(jnp.zeros((8, 128), F32) for _ in range(8)), unroll=2))
        for first_row, step in ((8, 2), (15, -2)):
            end = first_row + 4 * step
            for c in range(3):
                for kx, k, tiles in PARTS:
                    share = chain(c, tiles, end, step) * v0[c, first_row, tiles]
                    s = s_s[c, end, tiles]
                    m = s * s + (stencil_diag * smoothing + damping)
                    sums[7] = sums[7] + jnp.sum(m * share * v3[c, end - 6, tiles], axis=0)
        lane = lax.broadcasted_iota(jnp.int32, (1, 128), 1)
        out = jnp.zeros((1, 128), F32)
        for q in range(8):
            out = jnp.where(lane == q, jnp.sum(sums[q], keepdims=True), out)
        mom[...] = jnp.broadcast_to(out, mom.shape)
        s_copy.wait()
        for j in range(4):
            copy(j).wait()

    pl.run_scoped(
        prepare,
        pltpu.VMEM((8, 768, 128), F32),
        pltpu.VMEM((24, 16, 8, 128), F32),
    )
    pl.run_scoped(iterate, field(22), field(12))


def krylov(chunks, place, rowmask, peers):
    vmem = pl.BlockSpec(memory_space=pltpu.VMEM)
    hbm = pl.BlockSpec(memory_space=pltpu.HBM)

    return pl.pallas_call(
        krylov_kernel,
        out_shape=(
            jax.ShapeDtypeStruct((peers, 128), F32),
            jax.ShapeDtypeStruct((4, 3, 8, 16, 8, 128), F32),
            jax.ShapeDtypeStruct((3, 8, 16, 8, 128), F32),
            jax.ShapeDtypeStruct((2, 5, 128, 128), F32),
            jax.ShapeDtypeStruct((3, 8, 16, 8, 128), F32),
        ),
        in_specs=[pl.BlockSpec(memory_space=pltpu.SMEM)] * 2 + [vmem],
        out_specs=(vmem, hbm, hbm, vmem, vmem),
        scratch_shapes=[
            field(24),
            field(24),
            field(24),
            field(20),
            field(16),
            pltpu.SemaphoreType.DMA((6,)),
        ],
        compiler_params=pltpu.CompilerParams(vmem_limit_bytes=33 * 1024 * 1024),
        cost_estimate=pl.CostEstimate(flops=400_000_000, bytes_accessed=60_000_000, transcendentals=0),
        name="krylov",
    )(place, rowmask, chunks)


def ends_kernel(place, ends, inner, outer, out, rows):
    upper = lax.bitwise_and(place[0], 2) == 2
    both = [x[...].astype(F32).reshape(16, 1024) for x in (inner, outer)]
    for e in range(2):
        lines = jnp.where(upper, both[e], both[1 - e])
        for kz in range(8):
            rows[kz] = lines[:, kz * 128 : kz * 128 + 128]
        for slot, c in ((0, 0), (1, 2)):
            out[e, c] = ends[e, slot]
        for kx, k, tiles in PARTS:
            for b in range(WIDE):
                at = slice((tiles.start + b) * 8, (tiles.start + b) * 8 + 8)
                beyond = rows[FINE * b + k, pl.ds(kx, 8, stride=2), :]
                near = ends[e, 3, at, :]
                s = (near - beyond) * 0.5 if e == 0 else (beyond - near) * 0.5
                start = -s * ends[e, 4, at, :] / (s * s + (stencil_diag * smoothing + damping))
                out[e, 1, at, :] = ends[e, 2, at, :] * start


def outer_rows(ends, place, inner, outer):
    vmem = pl.BlockSpec(memory_space=pltpu.VMEM)
    return pl.pallas_call(
        ends_kernel,
        out_shape=jax.ShapeDtypeStruct((2, 3, 128, 128), F32),
        in_specs=[pl.BlockSpec(memory_space=pltpu.SMEM)] + [vmem] * 3,
        out_specs=vmem,
        scratch_shapes=[pltpu.VMEM((8, 16, 128), F32)],
        compiler_params=pltpu.CompilerParams(vmem_limit_bytes=4 * 1024 * 1024),
        name="outer_rows",
    )(place, ends, inner, outer)


def coefficients(m):
    def lam(k):
        if k == 0:
            return CENTRE * m[0] + HALF * m[1]
        return CENTRE * m[k] + (HALF / 2) * (m[k + 1] + m[k - 1])

    lams = [lam(k) for k in range(7)]
    rows = [[0.5 * (lams[i + j] + lams[abs(i - j)]) for j in range(4)] + [m[i]] for i in range(4)]
    for p in range(4):
        inverse = 1.0 / rows[p][p]
        for q in range(p + 1, 4):
            factor = rows[q][p] * inverse
            rows[q] = [rows[q][k] - factor * rows[p][k] if k > p else rows[q][k] for k in range(5)]
    part = [None] * 4
    for p in reversed(range(4)):
        value = rows[p][4]
        for q in range(p + 1, 4):
            value = value - rows[p][q] * part[q]
        part[p] = value / rows[p][p]
    rest = [1.0 - CENTRE * part[0] - (HALF / 2) * part[1]]
    rest.append(-CENTRE * part[1] - HALF * part[0] - (HALF / 2) * part[2])
    rest.append(-CENTRE * part[2] - (HALF / 2) * (part[1] + part[3]))
    rest.append(-CENTRE * part[3] - (HALF / 2) * part[2])
    rest.append(-(HALF / 2) * part[3])
    return part, rest


def combine_kernel(mom, v, last, s, outer, out, turn):
    line = jnp.sum(mom[...], axis=0, keepdims=True)
    lane = lax.broadcasted_iota(jnp.int32, (1, 128), 1)
    p = [jnp.sum(jnp.where(lane == k, line, 0.0), axis=1, keepdims=True) for k in range(8)]
    m = [p[0], p[1]] + [2.0 * p[k] - p[k % 2] for k in range(2, 8)]
    part, rest = coefficients(m)
    part = [jnp.broadcast_to(x, (8, 128)) for x in part]
    rest = [jnp.broadcast_to(x, (8, 128)) for x in rest]

    for c in range(3):

        def row(i, carry):
            for kx, k, tiles in PARTS:
                at = pl.ds(pl.multiple_of((kx * 8 + i) * 8, 8), 8)
                for b in range(WIDE):
                    vecs = [v[j, c, i, tiles.start + b] for j in range(4)] + [last[c, i, tiles.start + b]]
                    slope = s[c, i, tiles.start + b]
                    weight = slope * slope + (stencil_diag * smoothing + damping)
                    turn[c, 0, FINE * b + k, at, :] = sum(part[j] * vecs[j] for j in range(4))
                    turn[c, 1, FINE * b + k, at, :] = weight * sum(rest[j] * vecs[j] for j in range(5))
            return carry

        lax.fori_loop(0, 8, row, 0)
        for e, i in ((0, 0), (1, 7)):
            for kx, k, tiles in PARTS:
                at = slice((kx * 8 + i) * 8, (kx * 8 + i) * 8 + 8)
                for b in range(WIDE):
                    m = tiles.start + b
                    slope = s[c, i, m]
                    weight = slope * slope + (stencil_diag * smoothing + damping)
                    turn[c, 1, FINE * b + k, at, :] += weight * rest[4] * outer[e, c, m * 8 : m * 8 + 8, :]
        for q in range(2):
            for dest in range(8):
                for kz in range(8):
                    lanes = slice(kz * 128, kz * 128 + 128)
                    out[dest, q, c, :, lanes] = turn[c, q, kz, pl.ds(dest, 16, stride=8), :].astype(BF16)


def combine(moments, vectors, last, slopes, outer):
    vmem = pl.BlockSpec(memory_space=pltpu.VMEM)
    return pl.pallas_call(
        combine_kernel,
        out_shape=jax.ShapeDtypeStruct((8, 2, 3, 16, 1024), BF16),
        in_specs=[vmem] * 5,
        out_specs=vmem,
        scratch_shapes=[pltpu.VMEM((3, 2, 8, 128, 128), F32)],
        compiler_params=pltpu.CompilerParams(vmem_limit_bytes=24 * 1024 * 1024),
        name="combine",
    )(moments, vectors, last, slopes, outer)


def finish_kernel(flip, back, perm, sol, res, cells_s, sems):
    stores = []
    for c in range(3):
        lines = jnp.concatenate([back[src, q, c] for q in range(2) for src in range(8)], axis=0)
        lines = jnp.concatenate([lines[:, b * SPAN : b * SPAN + SPAN] for b in range(WIDE)], axis=0)
        cells = lax.dot_general(lines, perm[...], (((1,), (1,)), ((), ())), preferred_element_type=F32)
        for q, out in ((0, sol), (1, res)):
            for b in range(WIDE):
                for src in range(8):
                    rows = pl.ds(pl.multiple_of((src + flip[0] * (7 - 2 * src)) * 8, 8), 8)
                    for kx in range(2):
                        at = b * 256 + q * 128 + src * 16 + kx * 8
                        cells_s[q, c, kx, rows, b * SPAN : b * SPAN + SPAN] = cells[at : at + 8]
            stores.append(pltpu.make_async_copy(cells_s.at[q, c], out.at[c], sems.at[q, c]))
            stores[-1].start()
    for each in stores:
        each.wait()


def finish(back, flip, perm):
    shape = jax.ShapeDtypeStruct((3, 2, 64, 1024), F32)
    vmem = pl.BlockSpec(memory_space=pltpu.VMEM)
    hbm = pl.BlockSpec(memory_space=pltpu.HBM)
    return pl.pallas_call(
        finish_kernel,
        out_shape=(shape, shape),
        in_specs=[pl.BlockSpec(memory_space=pltpu.SMEM), vmem, vmem],
        out_specs=(hbm, hbm),
        scratch_shapes=[pltpu.VMEM((2, *shape.shape), F32), pltpu.SemaphoreType.DMA((2, 3))],
        compiler_params=pltpu.CompilerParams(vmem_limit_bytes=24 * 1024 * 1024),
        name="finish",
    )(flip, back, perm)


def exchange(cells, distance, inner):
    slabs, rows = lax.axis_size("slab"), lax.axis_size("row")

    def device(chunk):
        row, place = chunk // slabs, chunk % slabs
        return (place if row % 2 == 0 else slabs - 1 - place) * rows + row

    pairs = []
    for i in range(slabs * rows):
        low = (i // distance) % 2 == 0
        other = i + distance if low == inner else i - distance
        if 0 <= other < slabs * rows:
            pairs.append((device(i), device(other)))
    return lax.ppermute(cells, BOTH, pairs)


def per_device(moving, fixed, requests, footpoints, offset_x, offset_y, offset_z, fractions):
    depth, height, width = moving.shape
    perm = spread()
    block, slab = lax.axis_index("row"), lax.axis_index("slab")
    flip = block % 2
    start = block * height + (slab + flip * (7 - 2 * slab)) * 8 - 8
    peers, slots = requests.shape[2:]
    asked = jnp.pad(requests[0, 0], ((0, 0), (0, 128 - slots)))
    asked = lax.all_to_all(asked, BOTH, split_axis=0, concat_axis=0, tiled=True)
    outgoing = pick(asked, moving, slots)
    arrived = lax.all_to_all(outgoing, BOTH, split_axis=0, concat_axis=0, tiled=True)
    arrived = arrived.reshape(peers * slots, depth * TY, TZ)
    flip = flip.reshape(1)
    own = warp(
        arrived, footpoints[0, 0], offset_x[0, 0], offset_y[0, 0], offset_z[0, 0], fractions[0, 0], flip, fixed, perm
    )
    own = lax.all_to_all(own, "slab", split_axis=0, concat_axis=0, tiled=True)
    chunks = jnp.stack([exchange(own, 1, True), own, exchange(own, 1, False)])
    place = (slab + flip[0] * (7 - 2 * slab)).reshape(1)
    rows = start + jnp.arange(24, dtype=jnp.int32)
    rowmask = ((rows >= 0) & (rows < height * lax.axis_size("row"))).astype(F32)
    moments, vectors, slopes, ends, last = krylov(chunks, place, rowmask, peers)
    upper = place[0] // 2 % 2 == 1
    inwards = jnp.where(upper, own[:, 0:2, 0], own[:, 0:2, 7])
    outwards = jnp.where(upper, own[:, 0:2, 7], own[:, 0:2, 0])
    far = (exchange(inwards, 2, True), exchange(outwards, 2, False))
    moments, far = lax.optimization_barrier((moments, far))
    outer = outer_rows(ends, place, *far)
    moments, outer = lax.optimization_barrier((moments, outer))
    moments = lax.all_to_all(moments, BOTH, split_axis=0, concat_axis=0, tiled=True)
    back = combine(moments, vectors, last, slopes, outer)
    back = lax.all_to_all(back, "slab", split_axis=0, concat_axis=0, tiled=True)
    return finish(back, flip, perm)


def solution(mesh):
    return jax.shard_map(
        per_device,
        mesh=mesh,
        in_specs=(
            P("slab", "row", None),
            P("slab", "row", None),
            P("slab", "row", None, None),
            P("slab", "row", None, None),
            P("slab", "row", None),
            P("slab", "row", None),
            P("slab", "row", None),
            P("slab", "row", None, None),
        ),
        out_specs=(P(None, "slab", "row", None), P(None, "slab", "row", None)),
        check_vma=False,
    )
```

```python
import functools

import jax
import jax.numpy as jnp
from jax import lax
from jax.experimental import pallas as pl
from jax.experimental.pallas import tpu as pltpu
from jax.sharding import PartitionSpec as P

TY = 16
TZ = 128
ITERS = 4

smoothing = 0.02
damping = 0.1
stencil_diag = 42.0

LOW = 0.1
HIGH = 3.2
CENTRE = (HIGH + LOW) / 2
HALF = (HIGH - LOW) / 2
REACH = (smoothing / HALF) ** 4 * 8

FINE = 4
WIDE = 8 // FINE
SPAN = 128 * FINE

BOTH = ("slab", "row")
F32 = jnp.float32
BF16 = jnp.bfloat16


def spread():
    source = lax.broadcasted_iota(jnp.int32, (SPAN, SPAN), 0)
    target = lax.broadcasted_iota(jnp.int32, (SPAN, SPAN), 1)
    return (target == (source % FINE) * 128 + source // FINE).astype(BF16)


def pick_kernel(asked_hbm, moving, out, asked, block, buf, loads, stores):
    peers, slots, depth = buf.shape[:3]
    count = stores.shape[0]
    first = pltpu.make_async_copy(asked_hbm, asked, loads.at[0])
    second = pltpu.make_async_copy(moving, block, loads.at[1])
    first.start()
    second.start()
    first.wait()
    second.wait()

    def peer(p, carry):
        for slot in range(slots):
            number = asked[p * slots + slot]
            tile = jnp.maximum(number, 0)
            rows = pl.ds(pl.multiple_of(lax.shift_right_logical(tile, 3) * TY, TY), TY)
            lanes = pl.ds(pl.multiple_of(lax.bitwise_and(tile, 7) * TZ, TZ), TZ)
            for x in range(depth):
                cells = block[x, rows, lanes]
                buf[p, slot, x] = jnp.where(number >= 0, cells, jnp.zeros_like(cells))
        return carry

    part = peers // count
    sent = []
    for i in range(count):
        lax.fori_loop(i * part, (i + 1) * part, peer, 0, unroll=8)
        mine = pl.ds(i * part, part)
        sent.append(pltpu.make_async_copy(buf.at[mine], out.at[mine], stores.at[i]))
        sent[-1].start()
    for each in sent:
        each.wait()


def pick(asked, moving, slots):
    hbm = pl.BlockSpec(memory_space=pltpu.HBM)
    shape = (asked.shape[0], slots, moving.shape[0], TY, TZ)
    asked = asked[:, :slots].reshape(-1)
    return pl.pallas_call(
        pick_kernel,
        out_shape=jax.ShapeDtypeStruct(shape, BF16),
        in_specs=[hbm, hbm],
        out_specs=hbm,
        scratch_shapes=[
            pltpu.SMEM(asked.shape, jnp.int32),
            pltpu.VMEM(moving.shape, BF16),
            pltpu.VMEM(shape, BF16),
            pltpu.SemaphoreType.DMA((2,)),
            pltpu.SemaphoreType.DMA((4,)),
        ],
        compiler_params=pltpu.CompilerParams(vmem_limit_bytes=62 * 1024 * 1024),
        name="pick",
    )(asked, moving)


def warp_kernel(foot, ox, oy, oz, wts, flip, arrived, fixed, perm, out, nat):
    base_z = lax.broadcasted_iota(jnp.int32, (256, 128), 0) - lax.broadcasted_iota(jnp.int32, (256, 128), 1)
    ro = lax.broadcasted_iota(jnp.int32, (64, 128), 0)
    ci = lax.broadcasted_iota(jnp.int32, (64, 128), 1)
    same = (ro // 32 == ci // 64) & ((ro // 16) % 2 == (ci // 16) % 2)
    base_y = jnp.where(same, ((ci // 32) % 2) * 16 + ci % 16 - ro % 16, -1000)

    def band(base, shift, here, after):
        return jnp.where(base == shift, here, jnp.where(base == shift + 1, after, 0.0)).astype(BF16)

    def tile_row(j, carry):
        rows = pl.ds(pl.multiple_of(j * 16, 16), 16)
        firsts = []
        for k in range(8):
            t = j * 8 + k
            sides = []
            for c in range(2):
                corners = [arrived[foot[t * 8 + 4 * a + 2 * b + c]] for a in range(2) for b in range(2)]
                sides.append(jnp.concatenate(corners, axis=0))
            wz = band(base_z, oz[t], wts[t * 6 + 4], wts[t * 6 + 5])
            firsts.append(jnp.dot(jnp.concatenate(sides, axis=1), wz, preferred_element_type=F32).astype(BF16))
        seconds = []
        for k in range(8):
            t = j * 8 + k
            wy = band(base_y, oy[t], wts[t * 6 + 2], wts[t * 6 + 3])
            seconds.append(jnp.dot(wy, firsts[k], preferred_element_type=F32).astype(BF16).astype(F32))
        for k in range(8):
            t = j * 8 + k
            shift = ox[t]
            lanes = slice(k * 128, (k + 1) * 128)
            for xo in range(2):
                total = None
                for p in range(xo, xo + 3):
                    weight = jnp.where(
                        p - xo == shift, wts[t * 6], jnp.where(p - xo == shift + 1, wts[t * 6 + 1], 0.0)
                    )
                    term = weight * seconds[k][p * 16 : (p + 1) * 16]
                    total = term if total is None else total + term
                nat[xo, rows, lanes] = total.astype(BF16)
                nat[2 + xo, rows, lanes] = (total - fixed[xo, rows, lanes]).astype(BF16)
        return carry

    lax.fori_loop(0, 4, tile_row, 0)
    for b in range(WIDE):
        lanes = slice(b * SPAN, b * SPAN + SPAN)
        mixed = jnp.dot(nat[:, :, lanes].reshape(256, SPAN), perm[...], preferred_element_type=F32)
        for place in range(8):
            dest = place + flip[0] * (7 - 2 * place)
            for m in range(4):
                out[dest, m, :, lanes] = mixed[m * 64 + place * 8 : m * 64 + place * 8 + 8].astype(BF16)


def warp(arrived, footpoints, offset_x, offset_y, offset_z, fractions, flip, fixed, perm):
    near = lax.reduce_precision(1.0 - fractions, 8, 7)
    far = lax.reduce_precision(fractions, 8, 7)
    wts = jnp.stack([near, far], axis=-1).reshape(-1)
    smem = pl.BlockSpec(memory_space=pltpu.SMEM)
    vmem = pl.BlockSpec(memory_space=pltpu.VMEM)
    return pl.pallas_call(
        warp_kernel,
        out_shape=jax.ShapeDtypeStruct((8, 4, 8, 1024), BF16),
        in_specs=[smem] * 6 + [vmem] * 3,
        out_specs=vmem,
        scratch_shapes=[pltpu.VMEM((4, 64, 1024), BF16)],
        compiler_params=pltpu.CompilerParams(vmem_limit_bytes=10 * 1024 * 1024),
        name="warp",
    )(footpoints.reshape(-1), offset_x, offset_y, offset_z, wts, flip, arrived, fixed, perm)


PARTS = [
    (kx, k, slice(kx * 8 + k * WIDE, kx * 8 + k * WIDE + WIDE)) for kx in range(2) for k in range(FINE)
]


def edge_masks():
    sub = lax.broadcasted_iota(jnp.int32, (1, 8, 128), 1)
    lane = lax.broadcasted_iota(jnp.int32, (WIDE, 8, 128), 2)
    one = lambda flag: jnp.where(flag, 1.0, 0.0).astype(F32)
    return one(sub != 0), one(sub != 7), lane == 0, lane == 127


def load(ref, *at):
    return {(kx, k): ref[(*at, tiles)] for kx, k, tiles in PARTS}


def x_pair(v, kx, k, masks):
    other = v[1 - kx, k]
    if kx == 0:
        return pltpu.roll(other, 1, 1) * masks[0], other
    return other, pltpu.roll(other, 7, 1) * masks[1]


def z_pair(v, kx, k, masks):
    nothing = jnp.zeros((1, 8, 128), F32)
    if k > 0:
        before = v[kx, k - 1]
    else:
        turned = pltpu.roll(v[kx, FINE - 1], 1, 2)
        carried = jnp.concatenate([nothing, turned[: WIDE - 1]], axis=0) if WIDE > 1 else nothing
        before = jnp.where(masks[2], carried, turned)
    if k < FINE - 1:
        after = v[kx, k + 1]
    else:
        turned = pltpu.roll(v[kx, 0], 127, 2)
        carried = jnp.concatenate([turned[1:], nothing], axis=0) if WIDE > 1 else nothing
        after = jnp.where(masks[3], carried, turned)
    return before, after


def beside(v, kx, k, masks):
    x0, x1 = x_pair(v, kx, k, masks)
    z0, z1 = z_pair(v, kx, k, masks)
    return (x0 + x1) + (z0 + z1)


def field(rows):
    return pltpu.VMEM((3, rows, 16, 8, 128), F32)


def krylov_kernel(place, rowmask, chunks, mom, vout, sout, ends, v4, s_s, im_s, v0, v1, v2, sems):
    masks = edge_masks()

    def chain(c, tiles, end, step):
        one = im_s[c, end, tiles] * im_s[c, end - step, tiles]
        return one * (im_s[c, end - 2 * step, tiles] * im_s[c, end - 3 * step, tiles]) * REACH

    def prepare(d_s, w_s):
        odd = lax.bitwise_and(place[0], 1)
        sources = (2 - 2 * odd, 1, 2 * odd)
        for g in range(3):
            for src in range(8):
                lines = chunks[sources[g], src].astype(F32).reshape(32, 1024)
                for kz in range(8):
                    d_s[kz, src * 96 + g * 32 : src * 96 + g * 32 + 32, :] = lines[:, kz * 128 : kz * 128 + 128]

        def fetch(row, k, b):
            return d_s[FINE * b + k, pl.ds(row, 8, stride=96), :]

        def line(n, m):
            return lax.shift_right_logical(n, 3) * 32 + m * 8 + lax.bitwise_and(n, 7)

        def put_w(i, row_of):
            for kx, k, tiles in PARTS:
                for b in range(WIDE):
                    w_s[i, tiles.start + b] = fetch(row_of(kx), k, b)

        def fill(n, carry):
            put_w(n, lambda kx: line(n, kx))
            return carry

        lax.fori_loop(0, 24, fill, 0, unroll=4)

        def begin(n, carry):
            w = load(w_s, n)
            keep = rowmask[n]
            for kx, k, tiles in PARTS:
                diff = jnp.stack([fetch(line(n, 2 + kx), k, b) for b in range(WIDE)])
                xb, xa = x_pair(w, kx, k, masks)
                zb, za = z_pair(w, kx, k, masks)
                ys = w_s[n + 1, tiles] - w_s[n - 1, tiles]
                for c, s in enumerate(((xa - xb) * 0.5, ys * 0.5, (za - zb) * 0.5)):
                    im = keep / (s * s + (stencil_diag * smoothing + damping))
                    s_s[c, n, tiles] = s
                    im_s[c, n, tiles] = im
                    v0[c, n, tiles] = -s * diff * im
            return carry

        for c in range(3):
            for n in (0, 23):
                v0[c, n] = jnp.zeros((16, 8, 128), F32)
        lax.fori_loop(1, 23, begin, 0, unroll=2)

        for e, (edge, step) in enumerate(((0, 2), (23, -2))):
            w = load(w_s, edge)
            for kx, k, tiles in PARTS:
                lines = slice(tiles.start * 8, tiles.stop * 8)
                diff = jnp.stack([fetch(line(edge, 2 + kx), k, b) for b in range(WIDE)])
                xb, xa = x_pair(w, kx, k, masks)
                zb, za = z_pair(w, kx, k, masks)
                for slot, c, s in ((0, 0, (xa - xb) * 0.5), (1, 2, (za - zb) * 0.5)):
                    start = -s * diff / (s * s + (stencil_diag * smoothing + damping))
                    value = chain(c, tiles, edge + 4 * step, step) * start * rowmask[edge]
                    ends[e, slot, lines, :] = value.reshape(WIDE * 8, 128)
                ends[e, 2, lines, :] = (chain(1, tiles, edge + 4 * step, step) * rowmask[edge]).reshape(WIDE * 8, 128)
                ends[e, 3, lines, :] = w_s[edge + step // 2, tiles].reshape(WIDE * 8, 128)
                ends[e, 4, lines, :] = diff.reshape(WIDE * 8, 128)

    def iterate(u_s, v3):
        vs = [v0, v1, v2, v3, v4]

        def copy(j):
            return pltpu.make_async_copy(vs[j].at[:, pl.ds(8 - 2 * j, 8)], vout.at[j], sems.at[j])

        s_copy = pltpu.make_async_copy(s_s.at[:, pl.ds(8, 8)], sout, sems.at[5])
        s_copy.start()
        copy(0).start()

        for j in range(4):
            gain = (1.0 if j == 0 else 2.0) / HALF
            old, new = vs[j], vs[j + 1]
            off = 2 * j

            def first(n, carry):
                scale = rowmask[n] * (gain * smoothing)
                for c in range(3):
                    v = load(old, c, n - off)
                    for kx, k, tiles in PARTS:
                        total = beside(v, kx, k, masks) + (old[c, n - off - 1, tiles] + old[c, n - off + 1, tiles])
                        u_s[c, n - 1, tiles] = (6.0 * v[kx, k] - total) * scale
                return carry

            lax.fori_loop(off + 1, 23 - off, first, 0, unroll=2)

            def second(n, carry):
                dots = {}
                for kx, k, tiles in PARTS:
                    dot = s_s[0, n, tiles] * old[0, n - off, tiles]
                    dot = dot + s_s[1, n, tiles] * old[1, n - off, tiles]
                    dots[kx, k] = (dot + s_s[2, n, tiles] * old[2, n - off, tiles]) * gain
                for c in range(3):
                    u = load(u_s, c, n - 1)
                    for kx, k, tiles in PARTS:
                        total = beside(u, kx, k, masks) + (u_s[c, n - 2, tiles] + u_s[c, n, tiles])
                        v = old[c, n - off, tiles]
                        image = s_s[c, n, tiles] * dots[kx, k] + (6.0 * u[kx, k] - total) + (gain * damping) * v
                        value = im_s[c, n, tiles] * image - (gain * CENTRE) * v
                        if j > 0:
                            value = value - vs[j - 1][c, n - off + 2, tiles]
                        new[c, n - off - 2, tiles] = value
                return carry

            lax.fori_loop(off + 2, 22 - off, second, 0, unroll=2)
            if j < 3:
                copy(j + 1).start()

        def products(n, sums):
            sums = list(sums)
            for c in range(3):
                for kx, k, tiles in PARTS:
                    s = s_s[c, n, tiles]
                    m = s * s + (stencil_diag * smoothing + damping)
                    v = [vs[j][c, n - 2 * j, tiles] for j in range(5)]
                    for j in range(4):
                        t = m * v[j]
                        for q, other in ((2 * j, v[j]), (2 * j + 1, v[j + 1])):
                            sums[q] = sums[q] + jnp.sum(t * other, axis=0)
            return tuple(sums)

        sums = list(lax.fori_loop(8, 16, products, tuple(jnp.zeros((8, 128), F32) for _ in range(8)), unroll=2))
        for first_row, step in ((8, 2), (15, -2)):
            end = first_row + 4 * step
            for c in range(3):
                for kx, k, tiles in PARTS:
                    share = chain(c, tiles, end, step) * v0[c, first_row, tiles]
                    s = s_s[c, end, tiles]
                    m = s * s + (stencil_diag * smoothing + damping)
                    sums[7] = sums[7] + jnp.sum(m * share * v3[c, end - 6, tiles], axis=0)
        lane = lax.broadcasted_iota(jnp.int32, (1, 128), 1)
        out = jnp.zeros((1, 128), F32)
        for q in range(8):
            out = jnp.where(lane == q, jnp.sum(sums[q], keepdims=True), out)
        mom[...] = jnp.broadcast_to(out, mom.shape)
        s_copy.wait()
        for j in range(4):
            copy(j).wait()

    pl.run_scoped(
        prepare,
        pltpu.VMEM((8, 768, 128), F32),
        pltpu.VMEM((24, 16, 8, 128), F32),
    )
    pl.run_scoped(iterate, field(22), field(12))


def krylov(chunks, place, rowmask, peers):
    vmem = pl.BlockSpec(memory_space=pltpu.VMEM)
    hbm = pl.BlockSpec(memory_space=pltpu.HBM)

    return pl.pallas_call(
        krylov_kernel,
        out_shape=(
            jax.ShapeDtypeStruct((peers, 128), F32),
            jax.ShapeDtypeStruct((4, 3, 8, 16, 8, 128), F32),
            jax.ShapeDtypeStruct((3, 8, 16, 8, 128), F32),
            jax.ShapeDtypeStruct((2, 5, 128, 128), F32),
            jax.ShapeDtypeStruct((3, 8, 16, 8, 128), F32),
        ),
        in_specs=[pl.BlockSpec(memory_space=pltpu.SMEM)] * 2 + [vmem],
        out_specs=(vmem, hbm, hbm, vmem, vmem),
        scratch_shapes=[
            field(24),
            field(24),
            field(24),
            field(20),
            field(16),
            pltpu.SemaphoreType.DMA((6,)),
        ],
        compiler_params=pltpu.CompilerParams(vmem_limit_bytes=33 * 1024 * 1024),
        cost_estimate=pl.CostEstimate(flops=400_000_000, bytes_accessed=60_000_000, transcendentals=0),
        name="krylov",
    )(place, rowmask, chunks)


def ends_kernel(place, ends, inner, outer, out, rows):
    upper = lax.bitwise_and(place[0], 2) == 2
    both = [x[...].astype(F32).reshape(16, 1024) for x in (inner, outer)]
    for e in range(2):
        lines = jnp.where(upper, both[e], both[1 - e])
        for kz in range(8):
            rows[kz] = lines[:, kz * 128 : kz * 128 + 128]
        for slot, c in ((0, 0), (1, 2)):
            out[e, c] = ends[e, slot]
        for kx, k, tiles in PARTS:
            for b in range(WIDE):
                at = slice((tiles.start + b) * 8, (tiles.start + b) * 8 + 8)
                beyond = rows[FINE * b + k, pl.ds(kx, 8, stride=2), :]
                near = ends[e, 3, at, :]
                s = (near - beyond) * 0.5 if e == 0 else (beyond - near) * 0.5
                start = -s * ends[e, 4, at, :] / (s * s + (stencil_diag * smoothing + damping))
                out[e, 1, at, :] = ends[e, 2, at, :] * start


def outer_rows(ends, place, inner, outer):
    vmem = pl.BlockSpec(memory_space=pltpu.VMEM)
    return pl.pallas_call(
        ends_kernel,
        out_shape=jax.ShapeDtypeStruct((2, 3, 128, 128), F32),
        in_specs=[pl.BlockSpec(memory_space=pltpu.SMEM)] + [vmem] * 3,
        out_specs=vmem,
        scratch_shapes=[pltpu.VMEM((8, 16, 128), F32)],
        compiler_params=pltpu.CompilerParams(vmem_limit_bytes=4 * 1024 * 1024),
        name="outer_rows",
    )(place, ends, inner, outer)


def coefficients(m):
    def lam(k):
        if k == 0:
            return CENTRE * m[0] + HALF * m[1]
        return CENTRE * m[k] + (HALF / 2) * (m[k + 1] + m[k - 1])

    lams = [lam(k) for k in range(7)]
    rows = [[0.5 * (lams[i + j] + lams[abs(i - j)]) for j in range(4)] + [m[i]] for i in range(4)]
    for p in range(4):
        inverse = 1.0 / rows[p][p]
        for q in range(p + 1, 4):
            factor = rows[q][p] * inverse
            rows[q] = [rows[q][k] - factor * rows[p][k] if k > p else rows[q][k] for k in range(5)]
    part = [None] * 4
    for p in reversed(range(4)):
        value = rows[p][4]
        for q in range(p + 1, 4):
            value = value - rows[p][q] * part[q]
        part[p] = value / rows[p][p]
    rest = [1.0 - CENTRE * part[0] - (HALF / 2) * part[1]]
    rest.append(-CENTRE * part[1] - HALF * part[0] - (HALF / 2) * part[2])
    rest.append(-CENTRE * part[2] - (HALF / 2) * (part[1] + part[3]))
    rest.append(-CENTRE * part[3] - (HALF / 2) * part[2])
    rest.append(-(HALF / 2) * part[3])
    return part, rest


def combine_kernel(mom, v, last, s, outer, out, turn):
    line = jnp.sum(mom[...], axis=0, keepdims=True)
    lane = lax.broadcasted_iota(jnp.int32, (1, 128), 1)
    p = [jnp.sum(jnp.where(lane == k, line, 0.0), axis=1, keepdims=True) for k in range(8)]
    m = [p[0], p[1]] + [2.0 * p[k] - p[k % 2] for k in range(2, 8)]
    part, rest = coefficients(m)
    part = [jnp.broadcast_to(x, (8, 128)) for x in part]
    rest = [jnp.broadcast_to(x, (8, 128)) for x in rest]

    for c in range(3):

        def row(i, carry):
            for kx, k, tiles in PARTS:
                at = pl.ds(pl.multiple_of((kx * 8 + i) * 8, 8), 8)
                for b in range(WIDE):
                    vecs = [v[j, c, i, tiles.start + b] for j in range(4)] + [last[c, i, tiles.start + b]]
                    slope = s[c, i, tiles.start + b]
                    weight = slope * slope + (stencil_diag * smoothing + damping)
                    turn[c, 0, FINE * b + k, at, :] = sum(part[j] * vecs[j] for j in range(4))
                    turn[c, 1, FINE * b + k, at, :] = weight * sum(rest[j] * vecs[j] for j in range(5))
            return carry

        lax.fori_loop(0, 8, row, 0)
        for e, i in ((0, 0), (1, 7)):
            for kx, k, tiles in PARTS:
                at = slice((kx * 8 + i) * 8, (kx * 8 + i) * 8 + 8)
                for b in range(WIDE):
                    m = tiles.start + b
                    slope = s[c, i, m]
                    weight = slope * slope + (stencil_diag * smoothing + damping)
                    turn[c, 1, FINE * b + k, at, :] += weight * rest[4] * outer[e, c, m * 8 : m * 8 + 8, :]
        for q in range(2):
            for dest in range(8):
                for kz in range(8):
                    lanes = slice(kz * 128, kz * 128 + 128)
                    out[dest, q, c, :, lanes] = turn[c, q, kz, pl.ds(dest, 16, stride=8), :].astype(BF16)


def combine(moments, vectors, last, slopes, outer):
    vmem = pl.BlockSpec(memory_space=pltpu.VMEM)
    return pl.pallas_call(
        combine_kernel,
        out_shape=jax.ShapeDtypeStruct((8, 2, 3, 16, 1024), BF16),
        in_specs=[vmem] * 5,
        out_specs=vmem,
        scratch_shapes=[pltpu.VMEM((3, 2, 8, 128, 128), F32)],
        compiler_params=pltpu.CompilerParams(vmem_limit_bytes=24 * 1024 * 1024),
        name="combine",
    )(moments, vectors, last, slopes, outer)


def finish_kernel(flip, back, perm, sol, res, cells_s, sems):
    stores = []
    for c in range(3):
        lines = jnp.concatenate([back[src, q, c] for q in range(2) for src in range(8)], axis=0)
        lines = jnp.concatenate([lines[:, b * SPAN : b * SPAN + SPAN] for b in range(WIDE)], axis=0)
        cells = lax.dot_general(lines, perm[...], (((1,), (1,)), ((), ())), preferred_element_type=F32)
        for q, out in ((0, sol), (1, res)):
            for b in range(WIDE):
                for src in range(8):
                    rows = pl.ds(pl.multiple_of((src + flip[0] * (7 - 2 * src)) * 8, 8), 8)
                    for kx in range(2):
                        at = b * 256 + q * 128 + src * 16 + kx * 8
                        cells_s[q, c, kx, rows, b * SPAN : b * SPAN + SPAN] = cells[at : at + 8]
            stores.append(pltpu.make_async_copy(cells_s.at[q, c], out.at[c], sems.at[q, c]))
            stores[-1].start()
    for each in stores:
        each.wait()


def finish(back, flip, perm):
    shape = jax.ShapeDtypeStruct((3, 2, 64, 1024), F32)
    vmem = pl.BlockSpec(memory_space=pltpu.VMEM)
    hbm = pl.BlockSpec(memory_space=pltpu.HBM)
    return pl.pallas_call(
        finish_kernel,
        out_shape=(shape, shape),
        in_specs=[pl.BlockSpec(memory_space=pltpu.SMEM), vmem, vmem],
        out_specs=(hbm, hbm),
        scratch_shapes=[pltpu.VMEM((2, *shape.shape), F32), pltpu.SemaphoreType.DMA((2, 3))],
        compiler_params=pltpu.CompilerParams(vmem_limit_bytes=24 * 1024 * 1024),
        name="finish",
    )(flip, back, perm)


def exchange(cells, distance, inner):
    slabs, rows = lax.axis_size("slab"), lax.axis_size("row")

    def device(chunk):
        row, place = chunk // slabs, chunk % slabs
        return (place if row % 2 == 0 else slabs - 1 - place) * rows + row

    pairs = []
    for i in range(slabs * rows):
        low = (i // distance) % 2 == 0
        other = i + distance if low == inner else i - distance
        if 0 <= other < slabs * rows:
            pairs.append((device(i), device(other)))
    return lax.ppermute(cells, BOTH, pairs)


def per_device(moving, fixed, requests, footpoints, offset_x, offset_y, offset_z, fractions):
    depth, height, width = moving.shape
    perm = spread()
    block, slab = lax.axis_index("row"), lax.axis_index("slab")
    flip = block % 2
    start = block * height + (slab + flip * (7 - 2 * slab)) * 8 - 8
    peers, slots = requests.shape[2:]
    asked = jnp.pad(requests[0, 0], ((0, 0), (0, 128 - slots)))
    asked = lax.all_to_all(asked, BOTH, split_axis=0, concat_axis=0, tiled=True)
    outgoing = pick(asked, moving, slots)
    arrived = lax.all_to_all(outgoing, BOTH, split_axis=0, concat_axis=0, tiled=True)
    arrived = arrived.reshape(peers * slots, depth * TY, TZ)
    flip = flip.reshape(1)
    own = warp(
        arrived, footpoints[0, 0], offset_x[0, 0], offset_y[0, 0], offset_z[0, 0], fractions[0, 0], flip, fixed, perm
    )
    own = lax.all_to_all(own, "slab", split_axis=0, concat_axis=0, tiled=True)
    chunks = jnp.stack([exchange(own, 1, True), own, exchange(own, 1, False)])
    place = (slab + flip[0] * (7 - 2 * slab)).reshape(1)
    rows = start + jnp.arange(24, dtype=jnp.int32)
    rowmask = ((rows >= 0) & (rows < height * lax.axis_size("row"))).astype(F32)
    moments, vectors, slopes, ends, last = krylov(chunks, place, rowmask, peers)
    upper = place[0] // 2 % 2 == 1
    inwards = jnp.where(upper, own[:, 0:2, 0], own[:, 0:2, 7])
    outwards = jnp.where(upper, own[:, 0:2, 7], own[:, 0:2, 0])
    far = (exchange(inwards, 2, True), exchange(outwards, 2, False))
    moments, far = lax.optimization_barrier((moments, far))
    outer = outer_rows(ends, place, *far)
    moments, outer = lax.optimization_barrier((moments, outer))
    moments = lax.all_to_all(moments, BOTH, split_axis=0, concat_axis=0, tiled=True)
    back = combine(moments, vectors, last, slopes, outer)
    back = lax.all_to_all(back, "slab", split_axis=0, concat_axis=0, tiled=True)
    return finish(back, flip, perm)


def solution(mesh):
    return jax.shard_map(
        per_device,
        mesh=mesh,
        in_specs=(
            P("slab", "row", None),
            P("slab", "row", None),
            P("slab", "row", None, None),
            P("slab", "row", None, None),
            P("slab", "row", None),
            P("slab", "row", None),
            P("slab", "row", None),
            P("slab", "row", None, None),
        ),
        out_specs=(P(None, "slab", "row", None), P(None, "slab", "row", None)),
        check_vma=False,
    )
```
